32 devices in a mesh: freq: 4 (over z), row: 4 (over y, core), col: 2 (over x).
Axes of the slice: x: 2, y: 2, z: 4, core: 2. Of those that a mesh axis runs over, the one named last changes fastest.
Arguments:
- b_pairs: bfloat16 [6144, 2048], P(('row', 'col'), 'freq'), may hold values from -2 to 2
- occ_index: int32 [2048], P('freq'), may hold values from 0 to 255
- vir_index: int32 [2048], P('freq'), may hold values from 0 to 1791
- occ_depth: float32 [256], replicated, may hold values from 0.2 to 20
- vir_height: float32 [1792], replicated, may hold values from 0.05 to 30
- omega: float32 [4], P('freq'), may hold values from 0.05 to 50
Outputs:
- polar: float32 [4, 4, 2, 768, 6144], P('freq', None, 'col', None, 'row')
The draws below stay inside these ranges and needn't reach their ends.
Inputs may be any that keep to these rules, and one draw needn't show every extreme that they name: `occ_index`: an occupied orbital number. `vir_index`: a virtual orbital number.
All inputs are finite; a program needn't handle non-finite values.
Results may differ from the reference program's by a relative error of at most 0.0027.
Values may be sent and summed in bfloat16 or wider, within the bound.
No kernel may reach another device: no remote copies, remote signals or barrier semaphores. Data moves between devices by JAX's collectives and lax.ppermute only.
A program may use at most 128 MiB of HBM per device.

```python
import math
import jax
import jax.numpy as jnp
from jax import lax

NAUX = 6144
NOCC = 256
NVIR = 1792
SPAN = 512
STEPS = 4
NPAIRS = 2048
N_FREQ = 4
N_ROW = 4
N_COL = 2


def place_ends(drawn, own_key, low, largest):
    longest = drawn.shape.index(max(drawn.shape))
    spots = []
    for shift in (0, 1):
        where = [jax.random.randint(jax.random.fold_in(own_key, axis), (), 0, length) for axis, length in enumerate(drawn.shape)]
        where[longest] = (where[longest] + shift) % drawn.shape[longest]
        spots.append(tuple(where))
    return drawn.at[spots[0]].set(low).at[spots[1]].set(largest)


def levels(stream_key, extent, shards, low, high):
    level, own = 1.0, jax.random.fold_in(stream_key, 6)
    for axis_at, blocks in shards:
        steps = jnp.exp(jax.random.uniform(jax.random.fold_in(own, axis_at), (blocks,), jnp.float32, low / len(shards), high / len(shards)))
        level = level * jnp.repeat(steps, extent[axis_at] // blocks).reshape([-1 if axis == axis_at else 1 for axis in range(len(extent))])
    return level


def scatter_about(own_key, extent, width, limit, cuts=(), kind=jnp.bfloat16):
    entries = jax.random.normal(own_key, extent, jnp.float32) * width
    if len(cuts) > 0:
        entries = levels(own_key, extent, cuts, -0.22, 0.18) * entries
    return jnp.clip(entries, min=-limit, max=limit).astype(kind)


def setup_inputs(seed: int = 0) -> dict:
    key_list = jax.random.split(jax.random.key(seed), 7)
    b_pairs = scatter_about(key_list[0], (NAUX, NPAIRS), 0.125, 2.0, ((0, 8), (1, 4)))
    occ_index = place_ends(jax.random.randint(key_list[1], (NPAIRS,), 0, NOCC), jax.random.fold_in(key_list[1], 1), 0, NOCC - 1).astype(jnp.int32)
    vir_index = place_ends(jax.random.randint(key_list[2], (NPAIRS,), 0, NVIR), jax.random.fold_in(key_list[2], 1), 0, NVIR - 1).astype(jnp.int32)
    occ_depth = jnp.clip(jnp.exp(jax.random.uniform(key_list[3], (NOCC,), jnp.float32, math.log(0.2), math.log(20.0))), 0.2, 20.0)
    vir_height = jnp.clip(jnp.exp(jax.random.uniform(key_list[4], (NVIR,), jnp.float32, math.log(0.05), math.log(30.0))), 0.05, 30.0)
    omega = jnp.clip(jnp.exp(math.log(50.0) - 6.9077553 * jax.random.uniform(key_list[5], (N_FREQ,), jnp.float32) ** levels(key_list[5], (N_FREQ,), ((0, 4),), -0.2, 0.2)), 0.05, 50.0)
    return {"b_pairs": b_pairs, "occ_index": occ_index, "vir_index": vir_index, "occ_depth": occ_depth, "vir_height": vir_height, "omega": omega}


def reference(b_pairs, occ_index, vir_index, occ_depth, vir_height, omega):
    def one_group(group):
        square = omega[group] * omega[group]
        total = jnp.zeros((NAUX, NAUX), jnp.float32)
        for step in range(STEPS):
            source = ((group - step) % N_FREQ).astype(jnp.int32)
            start = (source * SPAN).astype(jnp.int32)
            block = lax.dynamic_slice_in_dim(b_pairs, start, SPAN, 1)
            occ_part = lax.dynamic_slice_in_dim(occ_index, start, SPAN, 0)
            vir_part = lax.dynamic_slice_in_dim(vir_index, start, SPAN, 0)
            gap = vir_height[vir_part] + occ_depth[occ_part]
            weight = 4.0 * gap / (gap * gap + square)
            weighted = (block.astype(jnp.float32) * weight[None, :]).astype(jnp.bfloat16)
            total = total + lax.dot_general(block, weighted, (((1,), (1,)), ((), ())), preferred_element_type=jnp.float32)
        return total.reshape(N_ROW, N_COL, NAUX // (N_ROW * N_COL), NAUX)

    return lax.map(one_group, jnp.arange(N_FREQ, dtype=jnp.int32))
```

```python
import functools

import jax
import jax.numpy as jnp
from jax import lax
from jax.experimental import pallas as pl
from jax.experimental.pallas import tpu as pltpu
from jax.sharding import PartitionSpec as P

STEPS = 4
PIECES = 6


def from_behind(value, axis, by):
    peers = lax.axis_size(axis)
    return lax.ppermute(value, axis, [(i, (i + by) % peers) for i in range(peers)])


def contract_pairs(left, right):
    return lax.dot_general(
        left, right, (((1,), (1,)), ((), ())), preferred_element_type=jnp.float32
    )


def ring_device(b_pairs, occ_index, vir_index, occ_depth, vir_height, omega):
    square = omega[0] * omega[0]
    n_row = lax.axis_size("row")
    n_col = lax.axis_size("col")
    sub_width = b_pairs.shape[0]
    total = jnp.zeros((sub_width * n_row, sub_width * n_col), jnp.float32)
    left = lax.all_gather(b_pairs, "col", axis=0, tiled=True)
    right = lax.all_gather(b_pairs, "row", axis=0, tiled=True)
    occ_part = occ_index
    vir_part = vir_index
    for step in range(STEPS):
        gap = jnp.take(vir_height, vir_part) + jnp.take(occ_depth, occ_part)
        weight = 4.0 * gap / (gap * gap + square)
        total = total + contract_pairs(
            right, (left.astype(jnp.float32) * weight[None, :]).astype(jnp.bfloat16)
        )
        if step + 1 < STEPS:
            left, right, occ_part, vir_part = from_behind(
                (left, right, occ_part, vir_part), "freq", 1
            )
    return total.reshape(1, n_row, 1, sub_width, sub_width * n_col)


def across(even):
    pairs = []
    for row in range(4):
        for col in range(2):
            along_col = (row % 2 == 0) == even
            to = (row, 1 - col) if along_col else ((row + 2) % 4, col)
            pairs.append((row * 2 + col, to[0] * 2 + to[1]))
    return lambda value: lax.ppermute(value, ("row", "col"), pairs)


def along_line(core_0, core_1):
    pairs = [
        (a * 4 + y * 2 + core, b * 4 + y * 2 + core)
        for core, hops in enumerate((core_0, core_1))
        for y in range(2)
        for a, b in hops
    ]
    return lambda value: lax.ppermute(value, ("freq", "row"), pairs)


OUTER = ((0, 1), (1, 0), (2, 3), (3, 2))
INNER = ((1, 2), (2, 1))
TO_ENDS = ((1, 0), (2, 3))


def other_core(value):
    return lax.ppermute(value, "row", [(i, i ^ 1) for i in range(4)])


def look_up(table, index):
    hit = index[:, None] == lax.broadcasted_iota(jnp.int32, (1, table.shape[0]), 1)
    return jnp.sum(jnp.where(hit, table[None, :], 0.0), axis=1)


def tile_kernel(slots, fresh, tiles, sub, span, *refs):
    n = len(slots)
    place, weight = refs[:2]
    pieces = [refs[2 + PIECES * k : 2 + PIECES * (k + 1)] for k in range(n)]
    rest = list(refs[2 + PIECES * n :])
    if not fresh:
        rest.pop(0)
    out, rbuf, lraw, lbuf, obuf, rsem, lsem, osem, isem = rest
    core = place[0]

    def cols(k):
        return pl.ds(k * span, span)

    def to_right(k, which, src):
        return pltpu.make_async_copy(src, rbuf.at[which, :, cols(k)], rsem.at[which, k])

    def to_left(k, src):
        return pltpu.make_async_copy(src, lraw.at[:, cols(k)], lsem.at[k])

    for k, slot in enumerate(slots):
        op_a, op_b, xy_a, xy_b, cs_a, cs_b = pieces[k]
        if slot == 0:
            to_right(k, core, op_a).start()
            to_right(k, 1 - core, op_b).start()
            y_a, y_b = 3, 2
        else:
            to_right(k, 0, op_a).start()
            to_right(k, 1, op_b).start()
            y_a, y_b = 2, 3

        @pl.when(core == 0)
        def _():
            to_left(k, xy_a).start()
            to_right(k, y_a, cs_a).start()
            to_right(k, y_b, xy_b).start()

        @pl.when(core == 1)
        def _():
            to_left(k, xy_b).start()
            to_right(k, y_a, xy_a).start()
            to_right(k, y_b, cs_b).start()

    def window(m):
        i, j = tiles[m]
        col = pl.multiple_of(((place[1] + j) % 2) * sub, sub)
        return out.at[place[2 + i], :, pl.ds(col, sub)]

    def put(m):
        return pltpu.make_async_copy(obuf.at[m % 2], window(m), osem.at[m % 2])

    def get(m):
        return pltpu.make_async_copy(window(m), obuf.at[m % 2], isem.at[m % 2])

    if not fresh:
        get(0).start()
    ready = set()

    def await_right(i):
        if i not in ready:
            ready.add(i)
            for k in range(n):
                to_right(k, i, pieces[k][0]).wait()

    def weigh(j):
        if j == 0:
            await_right(0)
            await_right(1)
        for k in range(n):
            if j == 1:
                to_left(k, pieces[k][2]).wait()

            @pl.loop(0, sub // 128)
            def _(r):
                rows = pl.ds(pl.multiple_of(r * 128, 128), 128)
                raw = rbuf[core, rows, cols(k)] if j == 0 else lraw[rows, cols(k)]
                lbuf[j, rows, cols(k)] = (raw.astype(jnp.float32) * weight[k]).astype(
                    jnp.bfloat16
                )

    weighed = set()
    for m, (i, j) in enumerate(tiles):
        if j not in weighed:
            weighed.add(j)
            weigh(j)
        await_right(i)
        if fresh:
            if m >= 2:
                put(m - 2).wait()
        else:
            get(m).wait()
        part = contract_pairs(rbuf[i], lbuf[j])
        obuf[m % 2] = part if fresh else obuf[m % 2] + part
        put(m).start()
        if not fresh and m + 1 < len(tiles):
            if m >= 1:
                put(m - 1).wait()
            get(m + 1).start()
    for m in range(max(len(tiles) - 2, 0), len(tiles)):
        put(m).wait()


def add_tiles(slots, tiles, place, weight, pieces, total):
    fresh = total is None
    n = len(slots)
    sub, span = pieces[0][0].shape
    anywhere = pl.BlockSpec(memory_space=pl.ANY)
    operands = [place, weight] + [piece for slot in pieces for piece in slot]
    aliases = {}
    if not fresh:
        aliases = {len(operands): 0}
        operands.append(total)
    moved = len(tiles) * sub * sub * 4 * (1 if fresh else 2)
    return pl.pallas_call(
        functools.partial(tile_kernel, slots, fresh, tiles, sub, span),
        out_shape=jax.ShapeDtypeStruct((4, sub, 2 * sub), jnp.float32),
        in_specs=[
            pl.BlockSpec(memory_space=pltpu.SMEM),
            pl.BlockSpec(memory_space=pltpu.VMEM),
        ]
        + [anywhere] * (len(operands) - 2),
        out_specs=anywhere,
        input_output_aliases=aliases,
        scratch_shapes=[
            pltpu.VMEM((4, sub, n * span), jnp.bfloat16),
            pltpu.VMEM((sub, n * span), jnp.bfloat16),
            pltpu.VMEM((2, sub, n * span), jnp.bfloat16),
            pltpu.VMEM((2, sub, sub), jnp.float32),
            pltpu.SemaphoreType.DMA((4, n)),
            pltpu.SemaphoreType.DMA((n,)),
            pltpu.SemaphoreType.DMA((2,)),
            pltpu.SemaphoreType.DMA((2,)),
        ],
        cost_estimate=pl.CostEstimate(
            flops=2 * len(tiles) * sub * sub * span * n,
            bytes_accessed=moved + 5 * n * sub * span * 2,
            transcendentals=0,
        ),
        compiler_params=pltpu.CompilerParams(vmem_limit_bytes=32 * 1024 * 1024),
    )(*operands)


def line_device(b_pairs, occ_index, vir_index, occ_depth, vir_height, omega):
    group = lax.axis_index("freq")
    row = lax.axis_index("row")
    col = lax.axis_index("col")
    core = row % 2
    first = core == 0
    end = (group == 0) | (group == 3)
    sub, span = b_pairs.shape

    xy = [across(True), across(False)]
    own = b_pairs
    cross = [None] * 8
    cross[0] = xy[0](own)
    hop_0 = along_line(OUTER, INNER)(own)
    cross[1] = xy[1](own)
    hop_1 = along_line(INNER, OUTER)(own)
    own_swap = other_core(own)
    hop_2 = along_line(INNER, TO_ENDS)(hop_0)
    swap_0 = other_core(hop_0)
    op_2 = jnp.where(first, hop_0, swap_0)
    cross[2] = xy[0](op_2)
    hop_3 = along_line(TO_ENDS, INNER)(hop_1)
    swap_1 = other_core(hop_1)
    op_3 = jnp.where(first, swap_1, hop_1)
    cross[3] = xy[1](op_3)
    hop_4 = along_line(TO_ENDS, ())(hop_2)
    swap_2 = other_core(hop_2)
    op_4 = jnp.where(
        end, jnp.where(first, swap_2, hop_2), jnp.where(first, swap_0, hop_0)
    )
    cross[4] = xy[1](op_4)
    hop_5 = along_line((), TO_ENDS)(hop_3)
    swap_3 = other_core(hop_3)
    op_5 = jnp.where(
        end, jnp.where(first, hop_3, swap_3), jnp.where(first, hop_1, swap_1)
    )
    cross[5] = xy[0](op_5)
    swap_4 = other_core(hop_4)
    op_6 = jnp.where(
        end, jnp.where(first, hop_4, swap_4), jnp.where(first, hop_2, swap_2)
    )
    cross[6] = xy[0](op_6)
    swap_5 = other_core(hop_5)
    op_7 = jnp.where(
        end, jnp.where(first, swap_5, hop_5), jnp.where(first, swap_3, hop_3)
    )
    cross[7] = xy[1](op_7)
    cross_swap = [other_core(value) for value in cross]

    def slot(op_a, op_b, a, b):
        return op_a, op_b, cross[a], cross[b], cross_swap[a], cross_swap[b]

    slots = [
        slot(own, own_swap, 0, 1),
        slot(op_2, op_3, 2, 3),
        slot(op_5, op_4, 5, 4),
        slot(op_6, op_7, 6, 7),
    ]

    occ_index, vir_index, hop_0 = lax.optimization_barrier(
        (occ_index, vir_index, hop_0)
    )
    gap = look_up(vir_height, vir_index) + look_up(occ_depth, occ_index)
    gaps = jnp.stack([gap] + [from_behind(gap, "freq", by) for by in (1, 2, 3)])
    near = jnp.where(group < 2, 2, 1)
    far = jnp.where(group < 2, 3, 0)
    source = jnp.stack([group, group ^ 1, near, far])
    gaps = jnp.take(gaps, (group - source) % 4, axis=0)
    weight = (4.0 * gaps / (gaps * gaps + omega[0] * omega[0]))[:, None, :]

    y = row // 2
    place = jnp.stack(
        [core, col, y * 2, y * 2 + 1, (1 - y) * 2, (1 - y) * 2 + 1]
    ).astype(jnp.int32)
    tiles = tuple((i, j) for j in range(2) for i in range(4))
    total = add_tiles((0, 1, 2), tiles, place, weight[:3], slots[:3], None)
    total = add_tiles((3,), tiles, place, weight[3:], slots[3:], total)
    return total.reshape(1, 4, 1, sub, 2 * sub)


def solution(mesh):
    in_specs = (P(("row", "col"), "freq"), P("freq"), P("freq"), P(), P(), P("freq"))
    out_specs = P("freq", None, "col", None, "row")
    shape = tuple(mesh.shape[axis] for axis in ("freq", "row", "col"))
    per_device = line_device if shape == (4, 4, 2) else ring_device
    return jax.shard_map(
        per_device, mesh=mesh, in_specs=in_specs, out_specs=out_specs, check_vma=False
    )
```

```python
import functools

import jax
import jax.numpy as jnp
from jax import lax
from jax.experimental import pallas as pl
from jax.experimental.pallas import tpu as pltpu
from jax.sharding import PartitionSpec as P

STEPS = 4
PAUSE = 4.0


def from_behind(value, axis, by):
    peers = lax.axis_size(axis)
    return lax.ppermute(value, axis, [(i, (i + by) % peers) for i in range(peers)])


def contract_pairs(left, right):
    return lax.dot_general(
        left, right, (((1,), (1,)), ((), ())), preferred_element_type=jnp.float32
    )


def ring_device(b_pairs, occ_index, vir_index, occ_depth, vir_height, omega):
    square = omega[0] * omega[0]
    n_row = lax.axis_size("row")
    n_col = lax.axis_size("col")
    sub_width = b_pairs.shape[0]
    total = jnp.zeros((sub_width * n_row, sub_width * n_col), jnp.float32)
    left = lax.all_gather(b_pairs, "col", axis=0, tiled=True)
    right = lax.all_gather(b_pairs, "row", axis=0, tiled=True)
    occ_part = occ_index
    vir_part = vir_index
    for step in range(STEPS):
        gap = jnp.take(vir_height, vir_part) + jnp.take(occ_depth, occ_part)
        weight = 4.0 * gap / (gap * gap + square)
        total = total + contract_pairs(
            right, (left.astype(jnp.float32) * weight[None, :]).astype(jnp.bfloat16)
        )
        if step + 1 < STEPS:
            left, right, occ_part, vir_part = from_behind(
                (left, right, occ_part, vir_part), "freq", 1
            )
    return total.reshape(1, n_row, 1, sub_width, sub_width * n_col)


def across_col(value):
    return lax.ppermute(value, "col", [(0, 1), (1, 0)])


def across_row(value):
    return lax.ppermute(value, "row", [(i, (i + 2) % 4) for i in range(4)])


def along_line(core_0, core_1):
    pairs = [
        (a * 4 + y * 2 + core, b * 4 + y * 2 + core)
        for core, hops in enumerate((core_0, core_1))
        for y in range(2)
        for a, b in hops
    ]
    return lambda value: lax.ppermute(value, ("freq", "row"), pairs)


OUTER = ((0, 1), (1, 0), (2, 3), (3, 2))
INNER = ((0, 0), (1, 2), (2, 1), (3, 3))
TO_ENDS = ((0, 1), (1, 0), (2, 3), (3, 2))
STAY = ((0, 0), (1, 1), (2, 2), (3, 3))


def other_core(value):
    return lax.ppermute(value, "row", [(i, i ^ 1) for i in range(4)])


def split_rows(value):
    rows = []
    for _ in range(3):
        part = lax.reduce_precision(value, exponent_bits=8, mantissa_bits=7)
        value = value - part
        rows.append(part)
    rows = jnp.stack(rows).astype(jnp.bfloat16)
    return jnp.concatenate([rows, jnp.zeros((13, rows.shape[1]), jnp.bfloat16)])


def join_rows(rows):
    rows = rows[:3].astype(jnp.float32)
    return rows[0] + (rows[1] + rows[2])


def after(value, *earlier):
    return lax.optimization_barrier((value, earlier))[0]


def look_up(table, index):
    hit = index[:, None] == lax.broadcasted_iota(jnp.int32, (1, table.shape[0]), 1)
    return jnp.sum(jnp.where(hit, table[None, :], 0.0), axis=1)


def tile_kernel(fresh, tiles, rights, lefts, write, *refs):
    place, weight = refs[:2]
    blocks = dict(zip([("r", i) for i in rights] + [("l", j) for j in lefts], refs[2:]))
    if write:
        acc, out, weighted, sem = refs[-4:]
    else:
        acc, weighted = refs[-2:]
    sub = acc.shape[2]

    def put(m):
        i, j = tiles[m]
        col = pl.multiple_of(((place[0] + j) % 2) * sub, sub)
        window = out.at[place[1 + i], :, pl.ds(col, sub)]
        return pltpu.make_async_copy(acc.at[j, i], window, sem.at[m])

    ready = set()
    for m, (i, j) in enumerate(tiles):
        if j not in ready:
            ready.add(j)
            left = blocks["l", j]

            @pl.loop(0, sub // 128)
            def _(r):
                rows = pl.ds(pl.multiple_of(r * 128, 128), 128)
                value = left[rows, :].astype(jnp.float32) * weight[...]
                weighted[j, rows, :] = value.astype(jnp.bfloat16)

        part = contract_pairs(blocks["r", i][:sub, :], weighted[j])
        if fresh:
            acc[j, i] = part
        else:
            acc[j, i] += part
        if write:
            put(m).start()
    if write:
        for m in range(len(tiles)):
            put(m).wait()


def add_tiles(tiles, place, weight, right, left, acc, write=False, out=None, tokens=()):
    sub, span = left[0].shape
    fresh = acc is None
    rights = sorted({i for i, _ in tiles})
    lefts = sorted({j for _, j in tiles})
    near = pl.BlockSpec(memory_space=pltpu.VMEM)
    far = pl.BlockSpec(memory_space=pl.ANY)
    operands = [place, weight]
    in_specs = [pl.BlockSpec(memory_space=pltpu.SMEM), near]
    for block in [right[i] for i in rights] + [left[j] for j in lefts]:
        operands.append(pltpu.with_memory_space_constraint(block, pltpu.VMEM))
        in_specs.append(near)
    aliases = {}
    if not fresh:
        aliases[len(operands)] = 0
        operands.append(pltpu.with_memory_space_constraint(acc, pltpu.VMEM))
        in_specs.append(near)
    if out is not None:
        aliases[len(operands)] = 1
        operands.append(out)
        in_specs.append(far)
    for token in tokens:
        operands.append(token)
        in_specs.append(far)
    out_shape = [pltpu.VMEM((2, 4, sub, sub), jnp.float32)]
    out_specs = [near]
    scratch = [pltpu.VMEM((2, sub, span), jnp.bfloat16)]
    if write:
        out_shape.append(jax.ShapeDtypeStruct((4, sub, 2 * sub), jnp.float32))
        out_specs.append(far)
        scratch.append(pltpu.SemaphoreType.DMA((len(tiles),)))
    return pl.pallas_call(
        functools.partial(tile_kernel, fresh, tiles, rights, lefts, write),
        out_shape=out_shape,
        in_specs=in_specs,
        out_specs=out_specs,
        input_output_aliases=aliases,
        scratch_shapes=scratch,
        cost_estimate=pl.CostEstimate(
            flops=2 * len(tiles) * sub * sub * span,
            bytes_accessed=len(tiles) * sub * sub * 4 if write else 0,
            transcendentals=0,
        ),
        compiler_params=pltpu.CompilerParams(vmem_limit_bytes=12 * 1024 * 1024),
    )(*operands)


def mark_kernel(block, rows, marked, sem):
    copy = pltpu.make_async_copy(block, marked.at[: block.shape[0], :], sem)
    copy.start()
    marked[block.shape[0] :, :] = rows[...]
    copy.wait()


def mark(block, rows):
    shape = (block.shape[0] + rows.shape[0], block.shape[1])
    return pl.pallas_call(
        mark_kernel,
        out_shape=pltpu.VMEM(shape, block.dtype),
        in_specs=[
            pl.BlockSpec(memory_space=pl.ANY),
            pl.BlockSpec(memory_space=pltpu.VMEM),
        ],
        out_specs=pl.BlockSpec(memory_space=pltpu.VMEM),
        scratch_shapes=[pltpu.SemaphoreType.DMA],
        compiler_params=pltpu.CompilerParams(vmem_limit_bytes=1024 * 1024),
    )(block, rows)


def pause_kernel(*refs):
    refs[-1][...] = jnp.zeros_like(refs[-1])


def pause(value, micros, tokens):
    parts = value if isinstance(value, tuple) else (value,)
    token = pl.pallas_call(
        pause_kernel,
        out_shape=jax.ShapeDtypeStruct((8, 128), jnp.float32),
        in_specs=[pl.BlockSpec(memory_space=pltpu.VMEM)] * len(parts),
        out_specs=pl.BlockSpec(memory_space=pltpu.VMEM),
        cost_estimate=pl.CostEstimate(
            flops=int(micros * 1e9),
            bytes_accessed=int(micros * 3e6),
            transcendentals=0,
        ),
        compiler_params=pltpu.CompilerParams(vmem_limit_bytes=4 * 1024 * 1024),
    )(*[pltpu.with_memory_space_constraint(v, pltpu.VMEM) for v in parts])
    tokens.append(token)
    return after(value, token)


def line_device(b_pairs, occ_index, vir_index, occ_depth, vir_height, omega):
    group = lax.axis_index("freq")
    row = lax.axis_index("row")
    col = lax.axis_index("col")
    core = row % 2
    first = core == 0
    end = (group == 0) | (group == 3)
    sub, span = b_pairs.shape

    own = b_pairs
    x, y = [None] * 4, [None] * 4
    tokens = []
    x[0] = across_col(own)
    y[0] = across_row(own)
    own_swap = other_core(own)
    hop_0 = along_line(OUTER, INNER)(after(own, own_swap))

    occ_index, vir_index = after((occ_index, vir_index), own_swap)
    own_gap = look_up(vir_height, vir_index) + look_up(occ_depth, occ_index)
    marked = mark(own, split_rows(own_gap))
    hop_1 = along_line(INNER, OUTER)(marked)
    x[0], y[0] = pause((x[0], y[0]), PAUSE, tokens)

    def pick(at_end, inside):
        def rows(low, high):
            pairs = [
                [v[low:high] if v.shape[0] > low else v[:high - low] for v in pair]
                for pair in (at_end, inside)
            ]
            if at_end is inside:
                return jnp.where(first, *pairs[0])
            return jnp.where(
                end, jnp.where(first, *pairs[0]), jnp.where(first, *pairs[1])
            )

        block = rows(0, sub)
        return block, rows(sub, marked.shape[0])

    hop_2 = along_line(INNER, TO_ENDS)(after(hop_0, marked))
    hop_0 = pause(hop_0, PAUSE, tokens)
    hop_3 = along_line(TO_ENDS, INNER)(after(hop_1, x[0], y[0]))
    pair = (hop_0, hop_1)
    mine_1, rows_1 = pick(pair, pair)
    x[1] = across_col(mine_1)
    y[1] = across_row(mine_1)
    x[1], y[1] = pause((x[1], y[1]), PAUSE, tokens)
    swap_1 = other_core(mine_1)

    hop_4 = along_line(TO_ENDS, STAY)(hop_2)
    hop_2 = pause(hop_2, PAUSE, tokens)
    hop_5 = along_line(STAY, TO_ENDS)(after(hop_3, x[1], y[1]))
    hop_0, hop_1 = after((hop_0, hop_1), mine_1)
    mine_2, rows_2 = pick((hop_3, hop_2), (hop_1, hop_0))
    x[2] = across_col(mine_2)
    y[2] = across_row(mine_2)
    x[2], y[2] = pause((x[2], y[2]), PAUSE, tokens)
    swap_2 = other_core(mine_2)

    hop_4 = pause(hop_4, PAUSE, tokens)
    hop_2, hop_3 = after((hop_2, hop_3), mine_2)
    mine_3, rows_3 = pick((hop_4, hop_5), (hop_2, hop_3))
    x[3] = across_col(mine_3)
    y[3] = across_row(mine_3)
    swap_3 = other_core(mine_3)

    def weigh(gap):
        return (4.0 * gap / (gap * gap + omega[0] * omega[0]))[None, :]

    def gap_of(rows, holder):
        return join_rows(jnp.where(core == holder, rows, other_core(rows)))

    rows_1 = after(rows_1, mine_1)
    rows_2 = after(rows_2, mine_2)
    rows_3 = after(rows_3, mine_3)
    weight = [
        weigh(own_gap),
        weigh(gap_of(rows_1, 1)),
        weigh(gap_of(rows_2, 0)),
        weigh(gap_of(rows_3, 1)),
    ]
    mine = [own, mine_1, mine_2, mine_3]
    swap = [own_swap, swap_1, swap_2, swap_3]

    place = jnp.stack([col, row, row ^ 1, row ^ 2, row ^ 3]).astype(jnp.int32)
    tiles = tuple((i, j) for j in range(2) for i in range(4))
    acc = None
    for k in range(3):
        place = after(place, mine[min(k + 2, 3)])
        right = (mine[k], swap[k], y[k], other_core(y[k]))
        (acc,) = add_tiles(tiles, place, weight[k], right, (mine[k], x[k]), acc)
    right = (mine[3], swap[3])
    acc, out = add_tiles(
        ((0, 0), (1, 0)), place, weight[3], right, (mine[3],), acc, write=True
    )
    x[3], y[3] = after((x[3], y[3]), acc)
    right = (mine[3], swap[3], y[3], other_core(y[3]))
    acc, out = add_tiles(
        ((0, 1), (1, 1), (2, 1), (2, 0)),
        place, weight[3], right, (mine[3], x[3]), acc, write=True, out=out,
    )
    _, out = add_tiles(
        ((3, 1), (3, 0)),
        place, weight[3], right, (mine[3], x[3]), acc, write=True, out=out,
        tokens=tokens,
    )
    return out.reshape(1, 4, 1, sub, 2 * sub)


def solution(mesh):
    in_specs = (P(("row", "col"), "freq"), P("freq"), P("freq"), P(), P(), P("freq"))
    out_specs = P("freq", None, "col", None, "row")
    shape = tuple(mesh.shape[axis] for axis in ("freq", "row", "col"))
    per_device = line_device if shape == (4, 4, 2) else ring_device
    return jax.shard_map(
        per_device, mesh=mesh, in_specs=in_specs, out_specs=out_specs, check_vma=False
    )
```

```python
import functools

import jax
import jax.numpy as jnp
from jax import lax
from jax.experimental import pallas as pl
from jax.experimental.pallas import tpu as pltpu
from jax.sharding import PartitionSpec as P

STEPS = 4
COSTS = (12, 1, 1)
LAGS = (8.0, 8.0, 4.0)


def from_behind(value, axis, by):
    peers = lax.axis_size(axis)
    return lax.ppermute(value, axis, [(i, (i + by) % peers) for i in range(peers)])


def contract_pairs(left, right):
    return lax.dot_general(
        left, right, (((1,), (1,)), ((), ())), preferred_element_type=jnp.float32
    )


def ring_device(b_pairs, occ_index, vir_index, occ_depth, vir_height, omega):
    square = omega[0] * omega[0]
    n_row = lax.axis_size("row")
    n_col = lax.axis_size("col")
    sub_width = b_pairs.shape[0]
    total = jnp.zeros((sub_width * n_row, sub_width * n_col), jnp.float32)
    left = lax.all_gather(b_pairs, "col", axis=0, tiled=True)
    right = lax.all_gather(b_pairs, "row", axis=0, tiled=True)
    occ_part = occ_index
    vir_part = vir_index
    for step in range(STEPS):
        gap = jnp.take(vir_height, vir_part) + jnp.take(occ_depth, occ_part)
        weight = 4.0 * gap / (gap * gap + square)
        total = total + contract_pairs(
            right, (left.astype(jnp.float32) * weight[None, :]).astype(jnp.bfloat16)
        )
        if step + 1 < STEPS:
            left, right, occ_part, vir_part = from_behind(
                (left, right, occ_part, vir_part), "freq", 1
            )
    return total.reshape(1, n_row, 1, sub_width, sub_width * n_col)


def across_col(value):
    return lax.ppermute(value, "col", [(0, 1), (1, 0)])


def across_row(value):
    return lax.ppermute(value, "row", [(i, (i + 2) % 4) for i in range(4)])


def along_line(hops):
    return lambda value: lax.ppermute(value, "freq", hops)


OUTER = ((0, 1), (1, 0), (2, 3), (3, 2))
INNER = ((0, 0), (1, 2), (2, 1), (3, 3))
TO_ENDS = ((0, 1), (1, 0), (2, 3), (3, 2))


def other_core(value):
    return lax.ppermute(value, "row", [(i, i ^ 1) for i in range(4)])


def join_rows(rows):
    rows = rows[:3].astype(jnp.float32)
    return rows[0] + (rows[1] + rows[2])


def after(value, *earlier):
    return lax.optimization_barrier((value, earlier))[0]


def look_up(long_table, long_index, table, index):
    size = long_table.shape[0]
    table = jnp.pad(table, (0, size - table.shape[0]))
    at = lax.broadcasted_iota(jnp.int32, (1, size), 1)
    first = jnp.where(long_index[:, None] == at, long_table[None, :], 0.0)
    second = jnp.where(index[:, None] == at, table[None, :], 0.0)
    return jnp.sum(first + second, axis=1)


def split_rows(value):
    rows = []
    for _ in range(3):
        part = lax.reduce_precision(value, exponent_bits=8, mantissa_bits=7)
        value = value - part
        rows.append(part)
    rows = jnp.stack(rows).astype(jnp.bfloat16)
    return jnp.concatenate([rows, jnp.zeros((13, rows.shape[1]), jnp.bfloat16)])


def in_vmem(value):
    return pltpu.with_memory_space_constraint(value, pltpu.VMEM)


def weigh_rows(weighted, left, weight):
    step = 128

    @pl.loop(0, weighted.shape[0] // step)
    def _(n):
        rows = pl.ds(pl.multiple_of(n * step, step), step)
        value = left[rows, :].astype(jnp.float32) * weight[...]
        weighted[rows, :] = value.astype(jnp.bfloat16)


def slot_kernel(fresh, token, weight, *refs):
    del token
    right, left = refs[:4], (refs[0], refs[4])
    acc, weighted = refs[-2:]
    sub = acc.shape[2]
    for j in range(2):
        weigh_rows(weighted.at[j], left[j], weight)
        for i in range(4):
            part = contract_pairs(right[i][:sub, :], weighted[j])
            if fresh:
                acc[j, i] = part
            else:
                acc[j, i] += part


def add_slot(sub, token, weight, right, left, acc, cost):
    span = left.shape[1]
    near = pl.BlockSpec(memory_space=pltpu.VMEM)
    operands = [token, weight] + [in_vmem(block) for block in (*right, left)]
    aliases = {}
    if acc is not None:
        aliases[len(operands)] = 0
        operands.append(in_vmem(acc))
    return pl.pallas_call(
        functools.partial(slot_kernel, acc is None),
        out_shape=pltpu.VMEM((2, 4, sub, sub), jnp.float32),
        in_specs=[near] * len(operands),
        out_specs=near,
        input_output_aliases=aliases,
        scratch_shapes=[pltpu.VMEM((2, sub, span), jnp.bfloat16)],
        cost_estimate=pl.CostEstimate(
            flops=16 * sub * sub * span * cost, bytes_accessed=0, transcendentals=0
        ),
        compiler_params=pltpu.CompilerParams(vmem_limit_bytes=12 * 1024 * 1024),
    )(*operands)


def finish_kernel(rights, lefts, jobs, n_in, *refs):
    place, weight = refs[:2]
    blocks = refs[2:n_in]
    acc, out, weighted, sem = refs[-4:]
    sub = acc.shape[2]

    def put(n):
        _, i, row, rows = rights[jobs[n][0]]
        _, j, first, cols = lefts[jobs[n][1]]
        column = pl.multiple_of(((place[0] + j) % 2) * sub + first, 128)
        window = out.at[place[1 + i], pl.ds(row, rows), pl.ds(column, cols)]
        part = acc.at[j, i, pl.ds(row, rows), pl.ds(first, cols)]
        return pltpu.make_async_copy(part, window, sem.at[n])

    ready = set()
    for n, (right, left) in enumerate(jobs):
        at, i, row, rows = rights[right]
        left_at, j, first, cols = lefts[left]
        if left not in ready:
            ready.add(left)
            part = weighted.at[j, pl.ds(first, cols), :]
            weigh_rows(part, blocks[left_at], weight)
        part = contract_pairs(blocks[at][:rows, :], weighted[j, first : first + cols, :])
        acc[j, i, row : row + rows, first : first + cols] += part
        put(n).start()
    for n in range(len(jobs)):
        put(n).wait()


def finish(place, weight, rights, lefts, jobs, acc, out, tokens=()):
    near = pl.BlockSpec(memory_space=pltpu.VMEM)
    far = pl.BlockSpec(memory_space=pltpu.HBM)
    sub, span = acc.shape[2], weight.shape[1]
    blocks, where = [], []
    for parts, used in ((rights, {r for r, _ in jobs}), (lefts, {l for _, l in jobs})):
        where.append({})
        for name in sorted(used):
            block, *at = parts[name]
            if not any(block is other for other in blocks):
                blocks.append(block)
            index = [block is other for other in blocks].index(True)
            where[-1][name] = (index, *at)
    operands = [place, weight] + [in_vmem(block) for block in blocks]
    n_in = len(operands)
    aliases = {n_in: 0}
    operands.append(in_vmem(acc))
    in_specs = [pl.BlockSpec(memory_space=pltpu.SMEM)] + [near] * n_in
    if out is not None:
        aliases[len(operands)] = 1
        operands.append(out)
        in_specs.append(far)
    operands += tokens
    in_specs += [near] * len(tokens)
    area = sum(where[0][r][-1] * where[1][l][-1] for r, l in jobs)
    return pl.pallas_call(
        functools.partial(finish_kernel, *where, jobs, n_in),
        out_shape=[
            pltpu.VMEM(acc.shape, acc.dtype),
            jax.ShapeDtypeStruct((4, sub, 2 * sub), jnp.float32),
        ],
        in_specs=in_specs,
        out_specs=[near, far],
        input_output_aliases=aliases,
        scratch_shapes=[
            pltpu.VMEM((2, sub, span), jnp.bfloat16),
            pltpu.SemaphoreType.DMA((len(jobs),)),
        ],
        cost_estimate=pl.CostEstimate(
            flops=2 * area * span, bytes_accessed=4 * area, transcendentals=0
        ),
        compiler_params=pltpu.CompilerParams(vmem_limit_bytes=12 * 1024 * 1024),
    )(*operands)


def mark_kernel(block, rows, marked, sem):
    part = block.shape[0] // 4
    copies = []
    for n in range(4):
        at = pl.ds(n * part, part)
        copies.append(pltpu.make_async_copy(block.at[at, :], marked.at[at, :], sem.at[n]))
    for copy in copies:
        copy.start()
    marked[block.shape[0] :, :] = rows[...]
    for copy in copies:
        copy.wait()


def mark(block, rows):
    shape = (block.shape[0] + rows.shape[0], block.shape[1])
    near = pl.BlockSpec(memory_space=pltpu.VMEM)
    return pl.pallas_call(
        mark_kernel,
        out_shape=pltpu.VMEM(shape, block.dtype),
        in_specs=[pl.BlockSpec(memory_space=pltpu.HBM), near],
        out_specs=near,
        scratch_shapes=[pltpu.SemaphoreType.DMA((4,))],
        compiler_params=pltpu.CompilerParams(vmem_limit_bytes=4 * 1024 * 1024),
    )(block, rows)


def pause_kernel(*refs):
    refs[-1][...] = jnp.zeros_like(refs[-1])


def lag(parts, micros, tokens):
    token = pl.pallas_call(
        pause_kernel,
        out_shape=jax.ShapeDtypeStruct((8, 128), jnp.float32),
        in_specs=[pl.BlockSpec(memory_space=pltpu.VMEM)] * len(parts),
        out_specs=pl.BlockSpec(memory_space=pltpu.VMEM),
        cost_estimate=pl.CostEstimate(
            flops=int(micros * 1e9),
            bytes_accessed=int(micros * 3e6),
            transcendentals=0,
        ),
        compiler_params=pltpu.CompilerParams(vmem_limit_bytes=4 * 1024 * 1024),
    )(*[pltpu.with_memory_space_constraint(v, pltpu.VMEM) for v in parts])
    tokens.append(token)
    return token


def gate_kernel(value, token, out):
    del value, token, out


def gate(value, token):
    near = pl.BlockSpec(memory_space=pltpu.VMEM)
    return pl.pallas_call(
        gate_kernel,
        out_shape=pltpu.VMEM(value.shape, value.dtype),
        in_specs=[near, near],
        out_specs=near,
        input_output_aliases={0: 0},
        cost_estimate=pl.CostEstimate(flops=1, bytes_accessed=1, transcendentals=0),
        compiler_params=pltpu.CompilerParams(vmem_limit_bytes=4 * 1024 * 1024),
    )(pltpu.with_memory_space_constraint(value, pltpu.VMEM), token)


def line_device(b_pairs, occ_index, vir_index, occ_depth, vir_height, omega):
    group = lax.axis_index("freq")
    row = lax.axis_index("row")
    col = lax.axis_index("col")
    end = (group == 0) | (group == 3)
    sub, span = b_pairs.shape

    tokens = []
    x, y = [None] * 4, [None] * 4
    own = b_pairs
    x[0] = across_col(own)
    y[0] = across_row(own)
    own_swap = other_core(own)

    gap = look_up(vir_height, vir_index, occ_depth, occ_index)
    marked = mark(own, split_rows(gap))
    near_1 = along_line(OUTER)(marked)
    near_2 = along_line(INNER)(marked)
    got = lag((near_2,), 0.1, tokens)
    place = jnp.stack([col, row, row ^ 1, row ^ 2, row ^ 3]).astype(jnp.int32)

    def add(mine, swap, x, y, acc, token, cost):
        right = (mine, swap, y, other_core(y))
        acc = add_slot(sub, token, weigh(mine), right, x, acc, cost)
        return acc, lag((acc, swap), 0.1, tokens)

    def weigh(block):
        gap = join_rows(block[sub:])
        return (4.0 * gap / (gap * gap + omega[0] * omega[0]))[None, :]

    here = lag((near_1, near_2), LAGS[2], tokens)
    mine_1 = jnp.where(after(group, here) >= 0, near_1, near_2)
    crossed = lag((mine_1,), 0.1, tokens)
    far_1 = along_line(TO_ENDS)(near_2)
    far_2 = along_line(INNER)(near_1)
    x[1] = across_col(mine_1)
    y[1] = across_row(mine_1)
    swap_1 = other_core(mine_1)
    acc, added = add(
        marked, own_swap, x[0], y[0], None, crossed, COSTS[0]
    )

    got_2 = lag((far_1, far_2, swap_1), LAGS[0], tokens)
    mine_2 = jnp.where(after(end, got, got_2, added), far_1, near_2)
    last = along_line(TO_ENDS)(far_2)
    x[2] = across_col(mine_2)
    y[2] = across_row(mine_2)
    swap_2 = other_core(mine_2)
    y[1] = gate(y[1], added)
    acc, added = add(
        mine_1, swap_1, x[1], y[1], acc, lag((mine_2,), 0.1, tokens), COSTS[1]
    )

    got = lag((last, swap_2), LAGS[1], tokens)
    mine_3 = jnp.where(after(end, got, added), last, far_2)
    cut = sub // 2
    halves = [(mine_3[:cut], 0), (mine_3[cut:sub], cut)]
    x[3] = [across_col(half) for half, _ in halves]
    y[3] = [across_row(half) for half, _ in halves]
    swap_3 = other_core(mine_3)
    acc, _ = add(
        mine_2, swap_2, x[2], y[2], acc, lag((mine_3,), 0.1, tokens), COSTS[2]
    )

    weight = weigh(mine_3)
    rights = {"own": (mine_3, 0, 0, sub), "swap": (swap_3, 1, 0, sub)}
    lefts = {"own": (mine_3, 0, 0, sub)}
    jobs = (("own", "own"), ("swap", "own"))
    acc, out = finish(place, weight, rights, lefts, jobs, acc, None)
    for n, (_, first) in enumerate(halves):
        token = lag((acc,), 0.1, tokens)
        left, right = gate(x[3][n], token), gate(y[3][n], token)
        here = after(place, lag((left, right), 16.0 if n == 0 else 4.0, tokens))
        rights |= {f"y{n}": (right, 2, first, cut), f"s{n}": (other_core(right), 3, first, cut)}
        lefts[f"x{n}"] = (left, 1, first, cut)
        if n == 0:
            jobs = (("own", "x0"), ("swap", "x0"), ("y0", "own"), ("y0", "x0"))
            jobs += (("s0", "own"), ("s0", "x0"))
            acc, out = finish(here, weight, rights, lefts, jobs, acc, out)
        else:
            jobs = (("own", "x1"), ("swap", "x1"), ("y1", "own"), ("y1", "x0"))
            jobs += (("y1", "x1"), ("y0", "x1"), ("s0", "x1"))
            acc, out = finish(here, weight, rights, lefts, jobs, acc, out)
            jobs = (("s1", "own"), ("s1", "x0"), ("s1", "x1"))
            acc, out = finish(place, weight, rights, lefts, jobs, acc, out, tokens)
    return out.reshape(1, 4, 1, sub, 2 * sub)


def solution(mesh):
    in_specs = (P(("row", "col"), "freq"), P("freq"), P("freq"), P(), P(), P("freq"))
    out_specs = P("freq", None, "col", None, "row")
    shape = tuple(mesh.shape[axis] for axis in ("freq", "row", "col"))
    per_device = line_device if shape == (4, 4, 2) else ring_device
    return jax.shard_map(
        per_device, mesh=mesh, in_specs=in_specs, out_specs=out_specs, check_vma=False
    )
```

```python
import functools

import jax
import jax.numpy as jnp
from jax import lax
from jax.experimental import pallas as pl
from jax.experimental.pallas import tpu as pltpu
from jax.sharding import PartitionSpec as P

STEPS = 4
COSTS = (12, 1, 1)
LAGS = (8.0, 8.0, 4.0)


def from_behind(value, axis, by):
    peers = lax.axis_size(axis)
    return lax.ppermute(value, axis, [(i, (i + by) % peers) for i in range(peers)])


def contract_pairs(left, right):
    return lax.dot_general(
        left, right, (((1,), (1,)), ((), ())), preferred_element_type=jnp.float32
    )


def ring_device(b_pairs, occ_index, vir_index, occ_depth, vir_height, omega):
    square = omega[0] * omega[0]
    n_row = lax.axis_size("row")
    n_col = lax.axis_size("col")
    sub_width = b_pairs.shape[0]
    total = jnp.zeros((sub_width * n_row, sub_width * n_col), jnp.float32)
    left = lax.all_gather(b_pairs, "col", axis=0, tiled=True)
    right = lax.all_gather(b_pairs, "row", axis=0, tiled=True)
    occ_part = occ_index
    vir_part = vir_index
    for step in range(STEPS):
        gap = jnp.take(vir_height, vir_part) + jnp.take(occ_depth, occ_part)
        weight = 4.0 * gap / (gap * gap + square)
        total = total + contract_pairs(
            right, (left.astype(jnp.float32) * weight[None, :]).astype(jnp.bfloat16)
        )
        if step + 1 < STEPS:
            left, right, occ_part, vir_part = from_behind(
                (left, right, occ_part, vir_part), "freq", 1
            )
    return total.reshape(1, n_row, 1, sub_width, sub_width * n_col)


def across_col(value):
    return lax.ppermute(value, "col", [(0, 1), (1, 0)])


def across_row(value):
    return lax.ppermute(value, "row", [(i, (i + 2) % 4) for i in range(4)])


def along_line(hops):
    return lambda value: lax.ppermute(value, "freq", hops)


OUTER = ((0, 1), (1, 0), (2, 3), (3, 2))
INNER = ((0, 0), (1, 2), (2, 1), (3, 3))
TO_ENDS = ((0, 1), (1, 0), (2, 3), (3, 2))


def other_core(value):
    return lax.ppermute(value, "row", [(i, i ^ 1) for i in range(4)])


def join_rows(rows):
    rows = rows[:3].astype(jnp.float32)
    return rows[0] + (rows[1] + rows[2])


def after(value, *earlier):
    return lax.optimization_barrier((value, earlier))[0]


def look_up(table, index):
    hit = index[:, None] == lax.broadcasted_iota(jnp.int32, (1, table.shape[0]), 1)
    return jnp.sum(jnp.where(hit, table[None, :], 0.0), axis=1)


def split_rows(value):
    rows = []
    for _ in range(3):
        part = lax.reduce_precision(value, exponent_bits=8, mantissa_bits=7)
        value = value - part
        rows.append(part)
    rows = jnp.stack(rows).astype(jnp.bfloat16)
    return jnp.concatenate([rows, jnp.zeros((13, rows.shape[1]), jnp.bfloat16)])


def in_vmem(value):
    return pltpu.with_memory_space_constraint(value, pltpu.VMEM)


def weigh_rows(weighted, left, weight):
    step = 128

    @pl.loop(0, weighted.shape[0] // step)
    def _(n):
        rows = pl.ds(pl.multiple_of(n * step, step), step)
        value = left[rows, :].astype(jnp.float32) * weight[...]
        weighted[rows, :] = value.astype(jnp.bfloat16)


def slot_kernel(fresh, token, weight, *refs):
    del token
    right, left = refs[:4], (refs[0], refs[4])
    acc, weighted = refs[-2:]
    sub = acc.shape[2]
    for j in range(2):
        weigh_rows(weighted.at[j], left[j], weight)
        for i in range(4):
            part = contract_pairs(right[i][:sub, :], weighted[j])
            if fresh:
                acc[j, i] = part
            else:
                acc[j, i] += part


def add_slot(sub, token, weight, right, left, acc, cost):
    span = left.shape[1]
    near = pl.BlockSpec(memory_space=pltpu.VMEM)
    operands = [token, weight] + [in_vmem(block) for block in (*right, left)]
    aliases = {}
    if acc is not None:
        aliases[len(operands)] = 0
        operands.append(in_vmem(acc))
    return pl.pallas_call(
        functools.partial(slot_kernel, acc is None),
        out_shape=pltpu.VMEM((2, 4, sub, sub), jnp.float32),
        in_specs=[near] * len(operands),
        out_specs=near,
        input_output_aliases=aliases,
        scratch_shapes=[pltpu.VMEM((2, sub, span), jnp.bfloat16)],
        cost_estimate=pl.CostEstimate(
            flops=16 * sub * sub * span * cost, bytes_accessed=0, transcendentals=0
        ),
        compiler_params=pltpu.CompilerParams(vmem_limit_bytes=12 * 1024 * 1024),
    )(*operands)


def finish_kernel(rights, lefts, fresh, jobs, n_in, *refs):
    place, weight = refs[:2]
    blocks = refs[2:n_in]
    acc, out, weighted, sem = refs[-4:]
    sub = acc.shape[2]

    def put(n):
        _, i, row, rows = rights[jobs[n][0]]
        _, j, first, cols = lefts[jobs[n][1]]
        column = pl.multiple_of(((place[0] + j) % 2) * sub + first, 128)
        window = out.at[place[1 + i], pl.ds(row, rows), pl.ds(column, cols)]
        part = acc.at[j, i, pl.ds(row, rows), pl.ds(first, cols)]
        return pltpu.make_async_copy(part, window, sem.at[n])

    ready = set()
    for n, (right, left) in enumerate(jobs):
        at, i, row, rows = rights[right]
        left_at, j, first, cols = lefts[left]
        if left in fresh and left not in ready:
            ready.add(left)
            part = weighted.at[j, pl.ds(first, cols), :]
            weigh_rows(part, blocks[left_at], weight)
        part = contract_pairs(blocks[at][:rows, :], weighted[j, first : first + cols, :])
        acc[j, i, row : row + rows, first : first + cols] += part
        put(n).start()
    for n in range(len(jobs)):
        put(n).wait()


def finish(place, weight, rights, lefts, fresh, jobs, state, tokens=()):
    near = pl.BlockSpec(memory_space=pltpu.VMEM)
    far = pl.BlockSpec(memory_space=pltpu.HBM)
    acc, weighted, out = state
    sub, span = acc.shape[2], weight.shape[1]
    blocks, where = [], []
    for parts, used in ((rights, {r for r, _ in jobs}), (lefts, {l for _, l in jobs})):
        where.append({})
        for name in sorted(used):
            block, *at = parts[name]
            if parts is lefts and name not in fresh:
                where[-1][name] = (None, *at)
                continue
            if not any(block is other for other in blocks):
                blocks.append(block)
            index = [block is other for other in blocks].index(True)
            where[-1][name] = (index, *at)
    operands = [place, weight] + [in_vmem(block) for block in blocks]
    n_in = len(operands)
    aliases = {n_in: 0}
    operands.append(in_vmem(acc))
    in_specs = [pl.BlockSpec(memory_space=pltpu.SMEM)] + [near] * n_in
    if out is not None:
        aliases |= {len(operands): 1, len(operands) + 1: 2}
        operands += [out, in_vmem(weighted)]
        in_specs += [far, near]
    operands += tokens
    in_specs += [near] * len(tokens)
    area = sum(where[0][r][-1] * where[1][l][-1] for r, l in jobs)
    return pl.pallas_call(
        functools.partial(finish_kernel, *where, fresh, jobs, n_in),
        out_shape=[
            pltpu.VMEM(acc.shape, acc.dtype),
            jax.ShapeDtypeStruct((4, sub, 2 * sub), jnp.float32),
            pltpu.VMEM((2, sub, span), jnp.bfloat16),
        ],
        in_specs=in_specs,
        out_specs=[near, far, near],
        input_output_aliases=aliases,
        scratch_shapes=[pltpu.SemaphoreType.DMA((len(jobs),))],
        cost_estimate=pl.CostEstimate(
            flops=2 * area * span, bytes_accessed=4 * area, transcendentals=0
        ),
        compiler_params=pltpu.CompilerParams(vmem_limit_bytes=12 * 1024 * 1024),
    )(*operands)


def mark_kernel(block, rows, marked, sem):
    part = block.shape[0] // 4
    copies = []
    for n in range(4):
        at = pl.ds(n * part, part)
        copies.append(pltpu.make_async_copy(block.at[at, :], marked.at[at, :], sem.at[n]))
    for copy in copies:
        copy.start()
    marked[block.shape[0] :, :] = rows[...]
    for copy in copies:
        copy.wait()


def mark(block, rows):
    shape = (block.shape[0] + rows.shape[0], block.shape[1])
    near = pl.BlockSpec(memory_space=pltpu.VMEM)
    return pl.pallas_call(
        mark_kernel,
        out_shape=pltpu.VMEM(shape, block.dtype),
        in_specs=[pl.BlockSpec(memory_space=pltpu.HBM), near],
        out_specs=near,
        scratch_shapes=[pltpu.SemaphoreType.DMA((4,))],
        compiler_params=pltpu.CompilerParams(vmem_limit_bytes=4 * 1024 * 1024),
    )(block, rows)


def pause_kernel(*refs):
    refs[-1][...] = jnp.zeros_like(refs[-1])


def lag(parts, micros, tokens):
    token = pl.pallas_call(
        pause_kernel,
        out_shape=jax.ShapeDtypeStruct((8, 128), jnp.float32),
        in_specs=[pl.BlockSpec(memory_space=pltpu.VMEM)] * len(parts),
        out_specs=pl.BlockSpec(memory_space=pltpu.VMEM),
        cost_estimate=pl.CostEstimate(
            flops=int(micros * 1e9),
            bytes_accessed=int(micros * 3e6),
            transcendentals=0,
        ),
        compiler_params=pltpu.CompilerParams(vmem_limit_bytes=4 * 1024 * 1024),
    )(*[pltpu.with_memory_space_constraint(v, pltpu.VMEM) for v in parts])
    tokens.append(token)
    return token


def gate_kernel(value, token, out):
    del value, token, out


def gate(value, token):
    near = pl.BlockSpec(memory_space=pltpu.VMEM)
    return pl.pallas_call(
        gate_kernel,
        out_shape=pltpu.VMEM(value.shape, value.dtype),
        in_specs=[near, near],
        out_specs=near,
        input_output_aliases={0: 0},
        cost_estimate=pl.CostEstimate(flops=1, bytes_accessed=1, transcendentals=0),
        compiler_params=pltpu.CompilerParams(vmem_limit_bytes=4 * 1024 * 1024),
    )(pltpu.with_memory_space_constraint(value, pltpu.VMEM), token)


def line_device(b_pairs, occ_index, vir_index, occ_depth, vir_height, omega):
    group = lax.axis_index("freq")
    row = lax.axis_index("row")
    col = lax.axis_index("col")
    end = (group == 0) | (group == 3)
    sub, span = b_pairs.shape

    tokens = []
    x, y = [None] * 4, [None] * 4
    own = b_pairs
    x[0] = across_col(own)
    y[0] = across_row(own)
    own_swap = other_core(own)

    gap = look_up(vir_height, vir_index) + look_up(occ_depth, occ_index)
    marked = mark(own, split_rows(gap))
    near_1 = along_line(OUTER)(marked)
    near_2 = along_line(INNER)(marked)
    got = lag((near_2,), 0.1, tokens)
    place = jnp.stack([col, row, row ^ 1, row ^ 2, row ^ 3]).astype(jnp.int32)

    def add(mine, swap, x, y, acc, token, cost):
        right = (mine, swap, y, other_core(y))
        acc = add_slot(sub, token, weigh(mine), right, x, acc, cost)
        return acc, lag((acc, swap), 0.1, tokens)

    def weigh(block):
        gap = join_rows(block[sub:])
        return (4.0 * gap / (gap * gap + omega[0] * omega[0]))[None, :]

    here = lag((near_1, near_2), LAGS[2], tokens)
    mine_1 = jnp.where(after(group, here) >= 0, near_1, near_2)
    crossed = lag((mine_1,), 0.1, tokens)
    far_1 = along_line(TO_ENDS)(near_2)
    far_2 = along_line(INNER)(near_1)
    x[1] = across_col(mine_1)
    y[1] = across_row(mine_1)
    swap_1 = other_core(mine_1)
    acc, added = add(
        marked, own_swap, x[0], y[0], None, crossed, COSTS[0]
    )

    got_2 = lag((far_1, far_2, swap_1), LAGS[0], tokens)
    mine_2 = jnp.where(after(end, got, got_2, added), far_1, near_2)
    last = along_line(TO_ENDS)(far_2)
    x[2] = across_col(mine_2)
    y[2] = across_row(mine_2)
    swap_2 = other_core(mine_2)
    y[1] = gate(y[1], added)
    acc, added = add(
        mine_1, swap_1, x[1], y[1], acc, lag((mine_2,), 0.1, tokens), COSTS[1]
    )

    got = lag((last, swap_2), LAGS[1], tokens)
    mine_3 = jnp.where(after(end, got, added), last, far_2)
    cut = sub // 2
    parts = [(mine_3[:cut], 0, cut), (mine_3[cut:sub], cut, sub - cut)]
    x[3] = [across_col(part) for part, _, _ in parts]
    y[3] = [across_row(part) for part, _, _ in parts]
    swap_3 = other_core(mine_3)
    acc, _ = add(
        mine_2, swap_2, x[2], y[2], acc, lag((mine_3,), 0.1, tokens), COSTS[2]
    )

    weight = weigh(mine_3)
    rights = {"own": (mine_3, 0, 0, sub), "swap": (swap_3, 1, 0, sub)}
    lefts = {"own": (mine_3, 0, 0, sub)}
    jobs = (("own", "own"), ("swap", "own"))
    state = finish(
        place, weight, rights, lefts, ("own",), jobs, (acc, None, None)
    )
    for n, (_, first, size) in enumerate(parts):
        acc, out, weighted = state
        token = lag((acc,), 0.1, tokens)
        left, right = gate(x[3][n], token), gate(y[3][n], token)
        here = after(place, lag((left, right), 16.0, tokens))
        rights[f"y{n}"] = (right, 2, first, size)
        rights[f"s{n}"] = (other_core(right), 3, first, size)
        lefts[f"x{n}"] = (left, 1, first, size)
        state = acc, weighted, out
        if n == 0:
            jobs = (("own", "x0"), ("swap", "x0"), ("y0", "own"), ("y0", "x0"))
            jobs += (("s0", "own"), ("s0", "x0"))
            state = finish(here, weight, rights, lefts, ("x0",), jobs, state)
        else:
            jobs = (("own", "x1"), ("swap", "x1"), ("y1", "own"), ("y1", "x0"))
            jobs += (("y1", "x1"), ("y0", "x1"), ("s0", "x1"))
            acc, out, weighted = finish(
                here, weight, rights, lefts, ("x1",), jobs, state
            )
            jobs = (("s1", "own"), ("s1", "x0"), ("s1", "x1"))
            state = acc, weighted, out
            _, out, _ = finish(place, weight, rights, lefts, (), jobs, state, tokens)
    return out.reshape(1, 4, 1, sub, 2 * sub)


def solution(mesh):
    in_specs = (P(("row", "col"), "freq"), P("freq"), P("freq"), P(), P(), P("freq"))
    out_specs = P("freq", None, "col", None, "row")
    shape = tuple(mesh.shape[axis] for axis in ("freq", "row", "col"))
    per_device = line_device if shape == (4, 4, 2) else ring_device
    return jax.shard_map(
        per_device, mesh=mesh, in_specs=in_specs, out_specs=out_specs, check_vma=False
    )
```

```python
import functools

import jax
import jax.numpy as jnp
from jax import lax
from jax.experimental import pallas as pl
from jax.experimental.pallas import tpu as pltpu
from jax.sharding import PartitionSpec as P

STEPS = 4
COSTS = (12, 1, 1)
LAGS = (8.0, 8.0, 4.0)


def from_behind(value, axis, by):
    peers = lax.axis_size(axis)
    return lax.ppermute(value, axis, [(i, (i + by) % peers) for i in range(peers)])


def contract_pairs(left, right):
    return lax.dot_general(
        left, right, (((1,), (1,)), ((), ())), preferred_element_type=jnp.float32
    )


def ring_device(b_pairs, occ_index, vir_index, occ_depth, vir_height, omega):
    square = omega[0] * omega[0]
    n_row = lax.axis_size("row")
    n_col = lax.axis_size("col")
    sub_width = b_pairs.shape[0]
    total = jnp.zeros((sub_width * n_row, sub_width * n_col), jnp.float32)
    left = lax.all_gather(b_pairs, "col", axis=0, tiled=True)
    right = lax.all_gather(b_pairs, "row", axis=0, tiled=True)
    occ_part = occ_index
    vir_part = vir_index
    for step in range(STEPS):
        gap = jnp.take(vir_height, vir_part) + jnp.take(occ_depth, occ_part)
        weight = 4.0 * gap / (gap * gap + square)
        total = total + contract_pairs(
            right, (left.astype(jnp.float32) * weight[None, :]).astype(jnp.bfloat16)
        )
        if step + 1 < STEPS:
            left, right, occ_part, vir_part = from_behind(
                (left, right, occ_part, vir_part), "freq", 1
            )
    return total.reshape(1, n_row, 1, sub_width, sub_width * n_col)


def across_col(value):
    return lax.ppermute(value, "col", [(0, 1), (1, 0)])


def across_row(value):
    return lax.ppermute(value, "row", [(i, (i + 2) % 4) for i in range(4)])


def along_line(hops):
    return lambda value: lax.ppermute(value, "freq", hops)


OUTER = ((0, 1), (1, 0), (2, 3), (3, 2))
INNER = ((0, 0), (1, 2), (2, 1), (3, 3))
TO_ENDS = ((0, 1), (1, 0), (2, 3), (3, 2))


def other_core(value):
    return lax.ppermute(value, "row", [(i, i ^ 1) for i in range(4)])


def join_rows(rows):
    rows = rows[:3].astype(jnp.float32)
    return rows[0] + (rows[1] + rows[2])


def after(value, *earlier):
    return lax.optimization_barrier((value, earlier))[0]


def look_up(table, index):
    hit = index[:, None] == lax.broadcasted_iota(jnp.int32, (1, table.shape[0]), 1)
    return jnp.sum(jnp.where(hit, table[None, :], 0.0), axis=1)


def split_rows(value):
    rows = []
    for _ in range(3):
        part = lax.reduce_precision(value, exponent_bits=8, mantissa_bits=7)
        value = value - part
        rows.append(part)
    rows = jnp.stack(rows).astype(jnp.bfloat16)
    return jnp.concatenate([rows, jnp.zeros((13, rows.shape[1]), jnp.bfloat16)])


def in_vmem(value):
    return pltpu.with_memory_space_constraint(value, pltpu.VMEM)


def weigh_rows(weighted, left, weight):
    step = 128

    @pl.loop(0, weighted.shape[0] // step)
    def _(n):
        rows = pl.ds(pl.multiple_of(n * step, step), step)
        value = left[rows, :].astype(jnp.float32) * weight[...]
        weighted[rows, :] = value.astype(jnp.bfloat16)


def slot_kernel(fresh, token, weight, *refs):
    del token
    right, left = refs[:4], (refs[0], refs[4])
    acc, weighted = refs[-2:]
    sub = acc.shape[2]
    for j in range(2):
        weigh_rows(weighted.at[j], left[j], weight)
        for i in range(4):
            part = contract_pairs(right[i][:sub, :], weighted[j])
            if fresh:
                acc[j, i] = part
            else:
                acc[j, i] += part


def add_slot(sub, token, weight, right, left, acc, cost):
    span = left.shape[1]
    near = pl.BlockSpec(memory_space=pltpu.VMEM)
    operands = [token, weight] + [in_vmem(block) for block in (*right, left)]
    aliases = {}
    if acc is not None:
        aliases[len(operands)] = 0
        operands.append(in_vmem(acc))
    return pl.pallas_call(
        functools.partial(slot_kernel, acc is None),
        out_shape=pltpu.VMEM((2, 4, sub, sub), jnp.float32),
        in_specs=[near] * len(operands),
        out_specs=near,
        input_output_aliases=aliases,
        scratch_shapes=[pltpu.VMEM((2, sub, span), jnp.bfloat16)],
        cost_estimate=pl.CostEstimate(
            flops=16 * sub * sub * span * cost, bytes_accessed=0, transcendentals=0
        ),
        compiler_params=pltpu.CompilerParams(vmem_limit_bytes=12 * 1024 * 1024),
    )(*operands)


def finish_kernel(rights, lefts, fresh, jobs, n_in, *refs):
    place, weight = refs[:2]
    blocks = refs[2:n_in]
    acc, out, weighted, sem = refs[-4:]
    sub = acc.shape[2]

    def put(n):
        _, i, row, rows = rights[jobs[n][0]]
        _, j, first, cols = lefts[jobs[n][1]]
        column = pl.multiple_of(((place[0] + j) % 2) * sub + first, 128)
        window = out.at[place[1 + i], pl.ds(row, rows), pl.ds(column, cols)]
        part = acc.at[j, i, pl.ds(row, rows), pl.ds(first, cols)]
        return pltpu.make_async_copy(part, window, sem.at[n])

    ready = set()
    for n, (right, left) in enumerate(jobs):
        at, i, row, rows = rights[right]
        left_at, j, first, cols = lefts[left]
        if left in fresh and left not in ready:
            ready.add(left)
            part = weighted.at[j, pl.ds(first, cols), :]
            weigh_rows(part, blocks[left_at], weight)
        part = contract_pairs(blocks[at][:rows, :], weighted[j, first : first + cols, :])
        acc[j, i, row : row + rows, first : first + cols] += part
        put(n).start()
    for n in range(len(jobs)):
        put(n).wait()


def finish(place, weight, rights, lefts, fresh, jobs, state, tokens=()):
    near = pl.BlockSpec(memory_space=pltpu.VMEM)
    far = pl.BlockSpec(memory_space=pltpu.HBM)
    acc, weighted, out = state
    sub, span = acc.shape[2], weight.shape[1]
    blocks, where = [], []
    for parts, used in ((rights, {r for r, _ in jobs}), (lefts, {l for _, l in jobs})):
        where.append({})
        for name in sorted(used):
            block, *at = parts[name]
            if parts is lefts and name not in fresh:
                where[-1][name] = (None, *at)
                continue
            if not any(block is other for other in blocks):
                blocks.append(block)
            index = [block is other for other in blocks].index(True)
            where[-1][name] = (index, *at)
    operands = [place, weight] + [in_vmem(block) for block in blocks]
    n_in = len(operands)
    aliases = {n_in: 0}
    operands.append(in_vmem(acc))
    in_specs = [pl.BlockSpec(memory_space=pltpu.SMEM)] + [near] * n_in
    if out is not None:
        aliases |= {len(operands): 1, len(operands) + 1: 2}
        operands += [out, in_vmem(weighted)]
        in_specs += [far, near]
    operands += tokens
    in_specs += [near] * len(tokens)
    area = sum(where[0][r][-1] * where[1][l][-1] for r, l in jobs)
    return pl.pallas_call(
        functools.partial(finish_kernel, *where, fresh, jobs, n_in),
        out_shape=[
            pltpu.VMEM(acc.shape, acc.dtype),
            jax.ShapeDtypeStruct((4, sub, 2 * sub), jnp.float32),
            pltpu.VMEM((2, sub, span), jnp.bfloat16),
        ],
        in_specs=in_specs,
        out_specs=[near, far, near],
        input_output_aliases=aliases,
        scratch_shapes=[pltpu.SemaphoreType.DMA((len(jobs),))],
        cost_estimate=pl.CostEstimate(
            flops=2 * area * span, bytes_accessed=4 * area, transcendentals=0
        ),
        compiler_params=pltpu.CompilerParams(vmem_limit_bytes=12 * 1024 * 1024),
    )(*operands)


def mark_kernel(block, rows, marked, sem):
    part = block.shape[0] // 4
    copies = []
    for n in range(4):
        at = pl.ds(n * part, part)
        copies.append(pltpu.make_async_copy(block.at[at, :], marked.at[at, :], sem.at[n]))
    for copy in copies:
        copy.start()
    marked[block.shape[0] :, :] = rows[...]
    for copy in copies:
        copy.wait()


def mark(block, rows):
    shape = (block.shape[0] + rows.shape[0], block.shape[1])
    near = pl.BlockSpec(memory_space=pltpu.VMEM)
    return pl.pallas_call(
        mark_kernel,
        out_shape=pltpu.VMEM(shape, block.dtype),
        in_specs=[pl.BlockSpec(memory_space=pltpu.HBM), near],
        out_specs=near,
        scratch_shapes=[pltpu.SemaphoreType.DMA((4,))],
        compiler_params=pltpu.CompilerParams(vmem_limit_bytes=4 * 1024 * 1024),
    )(block, rows)


def pause_kernel(*refs):
    refs[-1][...] = jnp.zeros_like(refs[-1])


def lag(parts, micros, tokens):
    token = pl.pallas_call(
        pause_kernel,
        out_shape=jax.ShapeDtypeStruct((8, 128), jnp.float32),
        in_specs=[pl.BlockSpec(memory_space=pl.ANY)] * len(parts),
        out_specs=pl.BlockSpec(memory_space=pltpu.VMEM),
        cost_estimate=pl.CostEstimate(
            flops=int(micros * 1e9),
            bytes_accessed=int(micros * 3e6),
            transcendentals=0,
        ),
        compiler_params=pltpu.CompilerParams(vmem_limit_bytes=4 * 1024 * 1024),
    )(*parts)
    tokens.append(token)
    return token


def gate_kernel(value, token, out):
    del value, token, out


def gate(value, token):
    near = pl.BlockSpec(memory_space=pltpu.VMEM)
    return pl.pallas_call(
        gate_kernel,
        out_shape=pltpu.VMEM(value.shape, value.dtype),
        in_specs=[near, near],
        out_specs=near,
        input_output_aliases={0: 0},
        cost_estimate=pl.CostEstimate(flops=1, bytes_accessed=1, transcendentals=0),
        compiler_params=pltpu.CompilerParams(vmem_limit_bytes=4 * 1024 * 1024),
    )(pltpu.with_memory_space_constraint(value, pltpu.VMEM), token)


def line_device(b_pairs, occ_index, vir_index, occ_depth, vir_height, omega):
    group = lax.axis_index("freq")
    row = lax.axis_index("row")
    col = lax.axis_index("col")
    end = (group == 0) | (group == 3)
    sub, span = b_pairs.shape

    tokens = []
    x, y = [None] * 4, [None] * 4
    own = b_pairs
    x[0] = across_col(own)
    y[0] = across_row(own)
    own_swap = other_core(own)

    gap = look_up(vir_height, vir_index) + look_up(occ_depth, occ_index)
    marked = mark(own, split_rows(gap))
    near_1 = along_line(OUTER)(marked)
    near_2 = along_line(INNER)(marked)
    near_2 = gate(near_2, lag((x[0], y[0]), 0.1, tokens))
    got = lag((near_2,), 0.1, tokens)
    place = jnp.stack([col, row, row ^ 1, row ^ 2, row ^ 3]).astype(jnp.int32)

    def add(mine, swap, x, y, acc, token, cost):
        right = (mine, swap, y, other_core(y))
        acc = add_slot(sub, token, weigh(mine), right, x, acc, cost)
        return acc, lag((acc, swap), 0.1, tokens)

    def weigh(block):
        gap = join_rows(block[sub:])
        return (4.0 * gap / (gap * gap + omega[0] * omega[0]))[None, :]

    swap_1 = other_core(near_1)
    here = lag((near_1, near_2, swap_1), LAGS[2], tokens)
    mine_1 = jnp.where(after(group, here) >= 0, near_1, near_2)
    crossed = lag((mine_1,), 0.1, tokens)
    far_1 = along_line(TO_ENDS)(near_2)
    far_2 = along_line(INNER)(near_1)
    x[1] = across_col(mine_1)
    y[1] = across_row(mine_1)
    acc, added = add(
        marked, own_swap, x[0], y[0], None, crossed, COSTS[0]
    )

    got_2 = lag((far_2,), LAGS[0], tokens)
    mine_2 = jnp.where(after(end, got, got_2, added), far_1, near_2)
    last = along_line(TO_ENDS)(far_2)
    x[2] = across_col(mine_2)
    y[2] = across_row(mine_2)
    swap_2 = other_core(mine_2)
    y[1] = gate(y[1], added)
    acc, added = add(
        mine_1, swap_1, x[1], y[1], acc, lag((mine_2,), 0.1, tokens), COSTS[1]
    )

    got = lag((last, swap_2, added), LAGS[1], tokens)
    mine_3 = jnp.where(after(end, got), last, far_2)
    cut = sub // 2
    parts = [(mine_3[:cut], 0, cut), (mine_3[cut:sub], cut, sub - cut)]
    x[3] = [across_col(part) for part, _, _ in parts]
    y[3] = [across_row(part) for part, _, _ in parts]
    swap_3 = other_core(mine_3)
    y[2] = gate(y[2], added)
    acc, _ = add(
        mine_2, swap_2, x[2], y[2], acc, lag((mine_3,), 0.1, tokens), COSTS[2]
    )

    weight = weigh(mine_3)
    rights = {"own": (mine_3, 0, 0, sub), "swap": (swap_3, 1, 0, sub)}
    lefts = {"own": (mine_3, 0, 0, sub)}
    jobs = (("own", "own"), ("swap", "own"))
    state = finish(
        place, weight, rights, lefts, ("own",), jobs, (acc, None, None)
    )
    for n, (_, first, size) in enumerate(parts):
        acc, out, weighted = state
        token = lag((acc,), 0.1, tokens)
        left, right = gate(x[3][n], token), gate(y[3][n], token)
        here = after(place, lag((left, right), 16.0, tokens))
        rights[f"y{n}"] = (right, 2, first, size)
        rights[f"s{n}"] = (other_core(right), 3, first, size)
        lefts[f"x{n}"] = (left, 1, first, size)
        state = acc, weighted, out
        if n == 0:
            jobs = (("own", "x0"), ("swap", "x0"), ("y0", "own"), ("y0", "x0"))
            jobs += (("s0", "own"), ("s0", "x0"))
            state = finish(here, weight, rights, lefts, ("x0",), jobs, state)
        else:
            jobs = (("own", "x1"), ("swap", "x1"), ("y1", "own"), ("y1", "x0"))
            jobs += (("y1", "x1"), ("y0", "x1"), ("s0", "x1"))
            acc, out, weighted = finish(
                here, weight, rights, lefts, ("x1",), jobs, state
            )
            jobs = (("s1", "own"), ("s1", "x0"), ("s1", "x1"))
            state = acc, weighted, out
            _, out, _ = finish(place, weight, rights, lefts, (), jobs, state, tokens)
    return out.reshape(1, 4, 1, sub, 2 * sub)


def solution(mesh):
    in_specs = (P(("row", "col"), "freq"), P("freq"), P("freq"), P(), P(), P("freq"))
    out_specs = P("freq", None, "col", None, "row")
    shape = tuple(mesh.shape[axis] for axis in ("freq", "row", "col"))
    per_device = line_device if shape == (4, 4, 2) else ring_device
    return jax.shard_map(
        per_device, mesh=mesh, in_specs=in_specs, out_specs=out_specs, check_vma=False
    )
```

```python
import functools

import jax
import jax.numpy as jnp
from jax import lax
from jax.experimental import pallas as pl
from jax.experimental.pallas import tpu as pltpu
from jax.sharding import PartitionSpec as P

STEPS = 4
COSTS = (12, 1, 1)
LAGS = (8.0, 8.0, 4.0)


def from_behind(value, axis, by):
    peers = lax.axis_size(axis)
    return lax.ppermute(value, axis, [(i, (i + by) % peers) for i in range(peers)])


def contract_pairs(left, right):
    return lax.dot_general(
        left, right, (((1,), (1,)), ((), ())), preferred_element_type=jnp.float32
    )


def ring_device(b_pairs, occ_index, vir_index, occ_depth, vir_height, omega):
    square = omega[0] * omega[0]
    n_row = lax.axis_size("row")
    n_col = lax.axis_size("col")
    sub_width = b_pairs.shape[0]
    total = jnp.zeros((sub_width * n_row, sub_width * n_col), jnp.float32)
    left = lax.all_gather(b_pairs, "col", axis=0, tiled=True)
    right = lax.all_gather(b_pairs, "row", axis=0, tiled=True)
    occ_part = occ_index
    vir_part = vir_index
    for step in range(STEPS):
        gap = jnp.take(vir_height, vir_part) + jnp.take(occ_depth, occ_part)
        weight = 4.0 * gap / (gap * gap + square)
        total = total + contract_pairs(
            right, (left.astype(jnp.float32) * weight[None, :]).astype(jnp.bfloat16)
        )
        if step + 1 < STEPS:
            left, right, occ_part, vir_part = from_behind(
                (left, right, occ_part, vir_part), "freq", 1
            )
    return total.reshape(1, n_row, 1, sub_width, sub_width * n_col)


def across_col(value):
    return lax.ppermute(value, "col", [(0, 1), (1, 0)])


def across_row(value):
    return lax.ppermute(value, "row", [(i, (i + 2) % 4) for i in range(4)])


def along_line(hops):
    return lambda value: lax.ppermute(value, "freq", hops)


OUTER = ((0, 1), (1, 0), (2, 3), (3, 2))
INNER = ((0, 0), (1, 2), (2, 1), (3, 3))
TO_ENDS = ((0, 1), (1, 0), (2, 3), (3, 2))


def other_core(value):
    return lax.ppermute(value, "row", [(i, i ^ 1) for i in range(4)])


def join_rows(rows):
    rows = rows[:3].astype(jnp.float32)
    return rows[0] + (rows[1] + rows[2])


def after(value, *earlier):
    return lax.optimization_barrier((value, earlier))[0]


def look_up(table, index):
    hit = index[None, :] == lax.broadcasted_iota(jnp.int32, (table.shape[0], 1), 0)
    return jnp.sum(jnp.where(hit, table[:, None], 0.0), axis=0)


def split_rows(value):
    rows = []
    for _ in range(3):
        part = lax.reduce_precision(value, exponent_bits=8, mantissa_bits=7)
        value = value - part
        rows.append(part)
    rows = jnp.stack(rows).astype(jnp.bfloat16)
    return jnp.concatenate([rows, jnp.zeros((13, rows.shape[1]), jnp.bfloat16)])


def in_vmem(value):
    return pltpu.with_memory_space_constraint(value, pltpu.VMEM)


def weigh_rows(weighted, left, weight):
    step = 128

    @pl.loop(0, weighted.shape[0] // step)
    def _(n):
        rows = pl.ds(pl.multiple_of(n * step, step), step)
        value = left[rows, :].astype(jnp.float32) * weight[...]
        weighted[rows, :] = value.astype(jnp.bfloat16)


def slot_kernel(fresh, token, weight, *refs):
    del token
    right, left = refs[:4], (refs[0], refs[4])
    acc, weighted = refs[-2:]
    sub = acc.shape[2]
    for j in range(2):
        weigh_rows(weighted.at[j], left[j], weight)
        for i in range(4):
            part = contract_pairs(right[i][:sub, :], weighted[j])
            if fresh:
                acc[j, i] = part
            else:
                acc[j, i] += part


def add_slot(sub, token, weight, right, left, acc, cost):
    span = left.shape[1]
    near = pl.BlockSpec(memory_space=pltpu.VMEM)
    operands = [token, weight] + [in_vmem(block) for block in (*right, left)]
    aliases = {}
    if acc is not None:
        aliases[len(operands)] = 0
        operands.append(in_vmem(acc))
    return pl.pallas_call(
        functools.partial(slot_kernel, acc is None),
        out_shape=pltpu.VMEM((2, 4, sub, sub), jnp.float32),
        in_specs=[near] * len(operands),
        out_specs=near,
        input_output_aliases=aliases,
        scratch_shapes=[pltpu.VMEM((2, sub, span), jnp.bfloat16)],
        cost_estimate=pl.CostEstimate(
            flops=16 * sub * sub * span * cost, bytes_accessed=0, transcendentals=0
        ),
        compiler_params=pltpu.CompilerParams(vmem_limit_bytes=12 * 1024 * 1024),
    )(*operands)


def finish_kernel(rights, lefts, fresh, jobs, n_in, *refs):
    place, weight = refs[:2]
    blocks = refs[2:n_in]
    acc, out, weighted, sem = refs[-4:]
    sub = acc.shape[2]

    def put(n):
        _, i, row, rows = rights[jobs[n][0]]
        _, j, first, cols = lefts[jobs[n][1]]
        column = pl.multiple_of(((place[0] + j) % 2) * sub + first, 128)
        window = out.at[place[1 + i], pl.ds(row, rows), pl.ds(column, cols)]
        part = acc.at[j, i, pl.ds(row, rows), pl.ds(first, cols)]
        return pltpu.make_async_copy(part, window, sem.at[n])

    ready = set()
    for n, (right, left) in enumerate(jobs):
        at, i, row, rows = rights[right]
        left_at, j, first, cols = lefts[left]
        if left in fresh and left not in ready:
            ready.add(left)
            part = weighted.at[j, pl.ds(first, cols), :]
            weigh_rows(part, blocks[left_at], weight)
        part = contract_pairs(blocks[at][:rows, :], weighted[j, first : first + cols, :])
        acc[j, i, row : row + rows, first : first + cols] += part
        put(n).start()
    for n in range(len(jobs)):
        put(n).wait()


def finish(place, weight, rights, lefts, fresh, jobs, state, tokens=()):
    near = pl.BlockSpec(memory_space=pltpu.VMEM)
    far = pl.BlockSpec(memory_space=pltpu.HBM)
    acc, weighted, out = state
    sub, span = acc.shape[2], weight.shape[1]
    blocks, where = [], []
    for parts, used in ((rights, {r for r, _ in jobs}), (lefts, {l for _, l in jobs})):
        where.append({})
        for name in sorted(used):
            block, *at = parts[name]
            if parts is lefts and name not in fresh:
                where[-1][name] = (None, *at)
                continue
            if not any(block is other for other in blocks):
                blocks.append(block)
            index = [block is other for other in blocks].index(True)
            where[-1][name] = (index, *at)
    operands = [place, weight] + [in_vmem(block) for block in blocks]
    n_in = len(operands)
    aliases = {n_in: 0}
    operands.append(in_vmem(acc))
    in_specs = [pl.BlockSpec(memory_space=pltpu.SMEM)] + [near] * n_in
    if out is not None:
        aliases |= {len(operands): 1, len(operands) + 1: 2}
        operands += [out, in_vmem(weighted)]
        in_specs += [far, near]
    operands += tokens
    in_specs += [near] * len(tokens)
    area = sum(where[0][r][-1] * where[1][l][-1] for r, l in jobs)
    return pl.pallas_call(
        functools.partial(finish_kernel, *where, fresh, jobs, n_in),
        out_shape=[
            pltpu.VMEM(acc.shape, acc.dtype),
            jax.ShapeDtypeStruct((4, sub, 2 * sub), jnp.float32),
            pltpu.VMEM((2, sub, span), jnp.bfloat16),
        ],
        in_specs=in_specs,
        out_specs=[near, far, near],
        input_output_aliases=aliases,
        scratch_shapes=[pltpu.SemaphoreType.DMA((len(jobs),))],
        cost_estimate=pl.CostEstimate(
            flops=2 * area * span, bytes_accessed=4 * area, transcendentals=0
        ),
        compiler_params=pltpu.CompilerParams(vmem_limit_bytes=12 * 1024 * 1024),
    )(*operands)


def mark_kernel(block, rows, marked, sem):
    part = block.shape[0] // 4
    copies = []
    for n in range(4):
        at = pl.ds(n * part, part)
        copies.append(pltpu.make_async_copy(block.at[at, :], marked.at[at, :], sem.at[n]))
    for copy in copies:
        copy.start()
    marked[block.shape[0] :, :] = rows[...]
    for copy in copies:
        copy.wait()


def mark(block, rows):
    shape = (block.shape[0] + rows.shape[0], block.shape[1])
    near = pl.BlockSpec(memory_space=pltpu.VMEM)
    return pl.pallas_call(
        mark_kernel,
        out_shape=pltpu.VMEM(shape, block.dtype),
        in_specs=[pl.BlockSpec(memory_space=pltpu.HBM), near],
        out_specs=near,
        scratch_shapes=[pltpu.SemaphoreType.DMA((4,))],
        compiler_params=pltpu.CompilerParams(vmem_limit_bytes=4 * 1024 * 1024),
    )(block, rows)


def pause_kernel(*refs):
    refs[-1][...] = jnp.zeros_like(refs[-1])


def lag(parts, micros, tokens):
    token = pl.pallas_call(
        pause_kernel,
        out_shape=jax.ShapeDtypeStruct((8, 128), jnp.float32),
        in_specs=[pl.BlockSpec(memory_space=pl.ANY)] * len(parts),
        out_specs=pl.BlockSpec(memory_space=pltpu.VMEM),
        cost_estimate=pl.CostEstimate(
            flops=int(micros * 1e9),
            bytes_accessed=int(micros * 3e6),
            transcendentals=0,
        ),
        compiler_params=pltpu.CompilerParams(vmem_limit_bytes=4 * 1024 * 1024),
    )(*parts)
    tokens.append(token)
    return token


def gate_kernel(value, token, out):
    del value, token, out


def gate(value, token):
    near = pl.BlockSpec(memory_space=pltpu.VMEM)
    return pl.pallas_call(
        gate_kernel,
        out_shape=pltpu.VMEM(value.shape, value.dtype),
        in_specs=[near, near],
        out_specs=near,
        input_output_aliases={0: 0},
        cost_estimate=pl.CostEstimate(flops=1, bytes_accessed=1, transcendentals=0),
        compiler_params=pltpu.CompilerParams(vmem_limit_bytes=4 * 1024 * 1024),
    )(pltpu.with_memory_space_constraint(value, pltpu.VMEM), token)


def line_device(b_pairs, occ_index, vir_index, occ_depth, vir_height, omega):
    group = lax.axis_index("freq")
    row = lax.axis_index("row")
    col = lax.axis_index("col")
    end = (group == 0) | (group == 3)
    sub, span = b_pairs.shape

    tokens = []
    x, y = [None] * 4, [None] * 4
    own = b_pairs
    x[0] = across_col(own)
    y[0] = across_row(own)
    own_swap = other_core(own)

    gap = look_up(vir_height, vir_index) + look_up(occ_depth, occ_index)
    marked = mark(own, split_rows(gap))
    near_1 = along_line(OUTER)(marked)
    near_2 = along_line(INNER)(marked)
    near_2 = gate(near_2, lag((x[0], y[0]), 0.1, tokens))
    got = lag((near_2,), 0.1, tokens)
    place = jnp.stack([col, row, row ^ 1, row ^ 2, row ^ 3]).astype(jnp.int32)

    def add(mine, swap, x, y, acc, token, cost):
        right = (mine, swap, y, other_core(y))
        acc = add_slot(sub, token, weigh(mine), right, x, acc, cost)
        return acc, lag((acc, swap), 0.1, tokens)

    def weigh(block):
        gap = join_rows(block[sub:])
        return (4.0 * gap / (gap * gap + omega[0] * omega[0]))[None, :]

    swap_1 = other_core(near_1)
    here = lag((near_1, near_2, swap_1), LAGS[2], tokens)
    mine_1 = jnp.where(after(group, here) >= 0, near_1, near_2)
    crossed = lag((mine_1,), 0.1, tokens)
    far_1 = along_line(TO_ENDS)(near_2)
    far_2 = along_line(INNER)(near_1)
    x[1] = across_col(mine_1)
    y[1] = across_row(mine_1)
    acc, added = add(
        marked, own_swap, x[0], y[0], None, crossed, COSTS[0]
    )

    got_2 = lag((far_2,), LAGS[0], tokens)
    mine_2 = jnp.where(after(end, got, got_2, added), far_1, near_2)
    last = along_line(TO_ENDS)(far_2)
    x[2] = across_col(mine_2)
    y[2] = across_row(mine_2)
    swap_2 = other_core(mine_2)
    y[1] = gate(y[1], added)
    acc, added = add(
        mine_1, swap_1, x[1], y[1], acc, lag((mine_2,), 0.1, tokens), COSTS[1]
    )

    got = lag((last, swap_2, added), LAGS[1], tokens)
    mine_3 = jnp.where(after(end, got), last, far_2)
    cut = sub * 2 // 3
    parts = [(mine_3[:cut], 0, cut), (mine_3[cut:sub], cut, sub - cut)]
    x[3] = [across_col(part) for part, _, _ in parts]
    y[3] = [across_row(part) for part, _, _ in parts]
    swap_3 = other_core(mine_3)
    y[2] = gate(y[2], added)
    acc, _ = add(
        mine_2, swap_2, x[2], y[2], acc, lag((mine_3,), 0.1, tokens), COSTS[2]
    )

    weight = weigh(mine_3)
    rights = {"own": (mine_3, 0, 0, sub), "swap": (swap_3, 1, 0, sub)}
    lefts = {"own": (mine_3, 0, 0, sub)}
    jobs = (("own", "own"), ("swap", "own"))
    state = finish(
        place, weight, rights, lefts, ("own",), jobs, (acc, None, None)
    )
    for n, (_, first, size) in enumerate(parts):
        acc, out, weighted = state
        token = lag((acc,), 0.1, tokens)
        left, right = gate(x[3][n], token), gate(y[3][n], token)
        here = after(place, lag((left, right), 16.0, tokens))
        rights[f"y{n}"] = (right, 2, first, size)
        rights[f"s{n}"] = (other_core(right), 3, first, size)
        lefts[f"x{n}"] = (left, 1, first, size)
        state = acc, weighted, out
        if n == 0:
            jobs = (("own", "x0"), ("swap", "x0"), ("y0", "own"), ("y0", "x0"))
            jobs += (("s0", "own"), ("s0", "x0"))
            state = finish(here, weight, rights, lefts, ("x0",), jobs, state)
        else:
            jobs = (("own", "x1"), ("swap", "x1"), ("y1", "own"), ("y1", "x0"))
            jobs += (("y1", "x1"), ("y0", "x1"), ("s0", "x1"))
            jobs += (("s1", "own"), ("s1", "x0"), ("s1", "x1"))
            _, out, _ = finish(
                here, weight, rights, lefts, ("x1",), jobs, state, tokens
            )
    return out.reshape(1, 4, 1, sub, 2 * sub)


def solution(mesh):
    in_specs = (P(("row", "col"), "freq"), P("freq"), P("freq"), P(), P(), P("freq"))
    out_specs = P("freq", None, "col", None, "row")
    shape = tuple(mesh.shape[axis] for axis in ("freq", "row", "col"))
    per_device = line_device if shape == (4, 4, 2) else ring_device
    return jax.shard_map(
        per_device, mesh=mesh, in_specs=in_specs, out_specs=out_specs, check_vma=False
    )
```

```python
import functools

import jax
import jax.numpy as jnp
from jax import lax
from jax.experimental import pallas as pl
from jax.experimental.pallas import tpu as pltpu
from jax.sharding import PartitionSpec as P

STEPS = 4
COSTS = (12, 1, 1)
LAGS = (8.0, 8.0, 4.0)


def from_behind(value, axis, by):
    peers = lax.axis_size(axis)
    return lax.ppermute(value, axis, [(i, (i + by) % peers) for i in range(peers)])


def contract_pairs(left, right):
    return lax.dot_general(
        left, right, (((1,), (1,)), ((), ())), preferred_element_type=jnp.float32
    )


def ring_device(b_pairs, occ_index, vir_index, occ_depth, vir_height, omega):
    square = omega[0] * omega[0]
    n_row = lax.axis_size("row")
    n_col = lax.axis_size("col")
    sub_width = b_pairs.shape[0]
    total = jnp.zeros((sub_width * n_row, sub_width * n_col), jnp.float32)
    left = lax.all_gather(b_pairs, "col", axis=0, tiled=True)
    right = lax.all_gather(b_pairs, "row", axis=0, tiled=True)
    occ_part = occ_index
    vir_part = vir_index
    for step in range(STEPS):
        gap = jnp.take(vir_height, vir_part) + jnp.take(occ_depth, occ_part)
        weight = 4.0 * gap / (gap * gap + square)
        total = total + contract_pairs(
            right, (left.astype(jnp.float32) * weight[None, :]).astype(jnp.bfloat16)
        )
        if step + 1 < STEPS:
            left, right, occ_part, vir_part = from_behind(
                (left, right, occ_part, vir_part), "freq", 1
            )
    return total.reshape(1, n_row, 1, sub_width, sub_width * n_col)


def across_col(value):
    return lax.ppermute(value, "col", [(0, 1), (1, 0)])


def across_row(value):
    return lax.ppermute(value, "row", [(i, (i + 2) % 4) for i in range(4)])


def along_line(hops):
    return lambda value: lax.ppermute(value, "freq", hops)


OUTER = ((0, 1), (1, 0), (2, 3), (3, 2))
INNER = ((0, 0), (1, 2), (2, 1), (3, 3))
TO_ENDS = ((0, 1), (1, 0), (2, 3), (3, 2))


def other_core(value):
    return lax.ppermute(value, "row", [(i, i ^ 1) for i in range(4)])


def join_rows(rows):
    rows = rows[:3].astype(jnp.float32)
    return rows[0] + (rows[1] + rows[2])


def after(value, *earlier):
    return lax.optimization_barrier((value, earlier))[0]


def look_up(table, index):
    hit = index[None, :] == lax.broadcasted_iota(jnp.int32, (table.shape[0], 1), 0)
    return jnp.sum(jnp.where(hit, table[:, None], 0.0), axis=0)


def split_rows(value):
    rows = []
    for _ in range(3):
        part = lax.reduce_precision(value, exponent_bits=8, mantissa_bits=7)
        value = value - part
        rows.append(part)
    rows = jnp.stack(rows).astype(jnp.bfloat16)
    return jnp.concatenate([rows, jnp.zeros((13, rows.shape[1]), jnp.bfloat16)])


def in_vmem(value):
    return pltpu.with_memory_space_constraint(value, pltpu.VMEM)


def weigh_rows(weighted, left, weight):
    step = 128

    @pl.loop(0, weighted.shape[0] // step)
    def _(n):
        rows = pl.ds(pl.multiple_of(n * step, step), step)
        value = left[rows, :].astype(jnp.float32) * weight[...]
        weighted[rows, :] = value.astype(jnp.bfloat16)


def slot_kernel(fresh, token, weight, *refs):
    del token
    right, left = refs[:4], (refs[0], refs[4])
    acc, weighted = refs[-2:]
    sub = acc.shape[2]
    for j in range(2):
        weigh_rows(weighted.at[j], left[j], weight)
        for i in range(4):
            part = contract_pairs(right[i][:sub, :], weighted[j])
            if fresh:
                acc[j, i] = part
            else:
                acc[j, i] += part


def add_slot(sub, token, weight, right, left, acc, cost):
    span = left.shape[1]
    near = pl.BlockSpec(memory_space=pltpu.VMEM)
    operands = [token, weight] + [in_vmem(block) for block in (*right, left)]
    aliases = {}
    if acc is not None:
        aliases[len(operands)] = 0
        operands.append(in_vmem(acc))
    return pl.pallas_call(
        functools.partial(slot_kernel, acc is None),
        out_shape=pltpu.VMEM((2, 4, sub, sub), jnp.float32),
        in_specs=[near] * len(operands),
        out_specs=near,
        input_output_aliases=aliases,
        scratch_shapes=[pltpu.VMEM((2, sub, span), jnp.bfloat16)],
        cost_estimate=pl.CostEstimate(
            flops=16 * sub * sub * span * cost, bytes_accessed=0, transcendentals=0
        ),
        compiler_params=pltpu.CompilerParams(vmem_limit_bytes=12 * 1024 * 1024),
    )(*operands)


def finish_kernel(rights, lefts, fresh, jobs, n_in, *refs):
    place, weight = refs[:2]
    blocks = refs[2:n_in]
    acc, out, weighted, sem = refs[-4:]
    sub = acc.shape[2]

    def put(n):
        _, i, row, rows = rights[jobs[n][0]]
        _, j, first, cols = lefts[jobs[n][1]]
        column = pl.multiple_of(((place[0] + j) % 2) * sub + first, 128)
        window = out.at[place[1 + i], pl.ds(row, rows), pl.ds(column, cols)]
        part = acc.at[j, i, pl.ds(row, rows), pl.ds(first, cols)]
        return pltpu.make_async_copy(part, window, sem.at[n])

    ready = set()
    for n, (right, left) in enumerate(jobs):
        at, i, row, rows = rights[right]
        left_at, j, first, cols = lefts[left]
        if left in fresh and left not in ready:
            ready.add(left)
            part = weighted.at[j, pl.ds(first, cols), :]
            weigh_rows(part, blocks[left_at], weight)
        part = contract_pairs(blocks[at][:rows, :], weighted[j, first : first + cols, :])
        acc[j, i, row : row + rows, first : first + cols] += part
        put(n).start()
    for n in range(len(jobs)):
        put(n).wait()


def finish(place, weight, rights, lefts, fresh, jobs, state, tokens=()):
    near = pl.BlockSpec(memory_space=pltpu.VMEM)
    far = pl.BlockSpec(memory_space=pltpu.HBM)
    acc, weighted, out = state
    sub, span = acc.shape[2], weight.shape[1]
    blocks, where = [], []
    for parts, used in ((rights, {r for r, _ in jobs}), (lefts, {l for _, l in jobs})):
        where.append({})
        for name in sorted(used):
            block, *at = parts[name]
            if parts is lefts and name not in fresh:
                where[-1][name] = (None, *at)
                continue
            if not any(block is other for other in blocks):
                blocks.append(block)
            index = [block is other for other in blocks].index(True)
            where[-1][name] = (index, *at)
    operands = [place, weight] + [in_vmem(block) for block in blocks]
    n_in = len(operands)
    aliases = {n_in: 0}
    operands.append(in_vmem(acc))
    in_specs = [pl.BlockSpec(memory_space=pltpu.SMEM)] + [near] * n_in
    if out is not None:
        aliases |= {len(operands): 1, len(operands) + 1: 2}
        operands += [out, in_vmem(weighted)]
        in_specs += [far, near]
    operands += tokens
    in_specs += [near] * len(tokens)
    area = sum(where[0][r][-1] * where[1][l][-1] for r, l in jobs)
    return pl.pallas_call(
        functools.partial(finish_kernel, *where, fresh, jobs, n_in),
        out_shape=[
            pltpu.VMEM(acc.shape, acc.dtype),
            jax.ShapeDtypeStruct((4, sub, 2 * sub), jnp.float32),
            pltpu.VMEM((2, sub, span), jnp.bfloat16),
        ],
        in_specs=in_specs,
        out_specs=[near, far, near],
        input_output_aliases=aliases,
        scratch_shapes=[pltpu.SemaphoreType.DMA((len(jobs),))],
        cost_estimate=pl.CostEstimate(
            flops=2 * area * span, bytes_accessed=4 * area, transcendentals=0
        ),
        compiler_params=pltpu.CompilerParams(vmem_limit_bytes=12 * 1024 * 1024),
    )(*operands)


def mark_kernel(block, rows, marked, sem):
    part = block.shape[0] // 8
    copies = []
    for n in range(8):
        at = pl.ds(n * part, part)
        copies.append(pltpu.make_async_copy(block.at[at, :], marked.at[at, :], sem.at[n]))
    for copy in copies:
        copy.start()
    marked[block.shape[0] :, :] = rows[...]
    for copy in copies:
        copy.wait()


def mark(block, rows):
    shape = (block.shape[0] + rows.shape[0], block.shape[1])
    near = pl.BlockSpec(memory_space=pltpu.VMEM)
    return pl.pallas_call(
        mark_kernel,
        out_shape=pltpu.VMEM(shape, block.dtype),
        in_specs=[pl.BlockSpec(memory_space=pltpu.HBM), near],
        out_specs=near,
        scratch_shapes=[pltpu.SemaphoreType.DMA((8,))],
        compiler_params=pltpu.CompilerParams(vmem_limit_bytes=4 * 1024 * 1024),
    )(block, rows)


def pause_kernel(*refs):
    refs[-1][...] = jnp.zeros_like(refs[-1])


def lag(parts, micros, tokens):
    token = pl.pallas_call(
        pause_kernel,
        out_shape=jax.ShapeDtypeStruct((8, 128), jnp.float32),
        in_specs=[pl.BlockSpec(memory_space=pl.ANY)] * len(parts),
        out_specs=pl.BlockSpec(memory_space=pltpu.VMEM),
        cost_estimate=pl.CostEstimate(
            flops=int(micros * 1e9),
            bytes_accessed=int(micros * 3e6),
            transcendentals=0,
        ),
        compiler_params=pltpu.CompilerParams(vmem_limit_bytes=4 * 1024 * 1024),
    )(*parts)
    tokens.append(token)
    return token


def gate_kernel(value, token, out):
    del value, token, out


def gate(value, token):
    near = pl.BlockSpec(memory_space=pltpu.VMEM)
    return pl.pallas_call(
        gate_kernel,
        out_shape=pltpu.VMEM(value.shape, value.dtype),
        in_specs=[near, near],
        out_specs=near,
        input_output_aliases={0: 0},
        cost_estimate=pl.CostEstimate(flops=1, bytes_accessed=1, transcendentals=0),
        compiler_params=pltpu.CompilerParams(vmem_limit_bytes=4 * 1024 * 1024),
    )(pltpu.with_memory_space_constraint(value, pltpu.VMEM), token)


def line_device(b_pairs, occ_index, vir_index, occ_depth, vir_height, omega):
    group = lax.axis_index("freq")
    row = lax.axis_index("row")
    col = lax.axis_index("col")
    end = (group == 0) | (group == 3)
    sub, span = b_pairs.shape

    tokens = []
    x, y = [None] * 4, [None] * 4
    own = b_pairs
    x[0] = across_col(own)
    y[0] = across_row(own)
    own_swap = other_core(own)

    gap = look_up(vir_height, vir_index) + look_up(occ_depth, occ_index)
    marked = mark(own, split_rows(gap))
    near_1 = along_line(OUTER)(marked)
    near_2 = along_line(INNER)(marked)
    near_2 = gate(near_2, lag((x[0], y[0]), 0.1, tokens))
    got = lag((near_2,), 0.1, tokens)
    place = jnp.stack([col, row, row ^ 1, row ^ 2, row ^ 3]).astype(jnp.int32)

    def add(mine, swap, x, y, acc, token, cost):
        right = (mine, swap, y, other_core(y))
        acc = add_slot(sub, token, weigh(mine), right, x, acc, cost)
        return acc, lag((acc, swap), 0.1, tokens)

    def weigh(block):
        gap = join_rows(block[sub:])
        return (4.0 * gap / (gap * gap + omega[0] * omega[0]))[None, :]

    swap_1 = other_core(near_1)
    here = lag((near_1, near_2, swap_1), LAGS[2], tokens)
    mine_1 = jnp.where(after(group, here) >= 0, near_1, near_2)
    crossed = lag((mine_1,), 0.1, tokens)
    far_1 = along_line(TO_ENDS)(near_2)
    far_2 = along_line(INNER)(near_1)
    x[1] = across_col(mine_1)
    y[1] = across_row(mine_1)
    acc, added = add(
        marked, own_swap, x[0], y[0], None, crossed, COSTS[0]
    )

    got_2 = lag((far_2,), LAGS[0], tokens)
    mine_2 = jnp.where(after(end, got, got_2, added), far_1, near_2)
    last = along_line(TO_ENDS)(far_2)
    x[2] = across_col(mine_2)
    y[2] = across_row(mine_2)
    swap_2 = other_core(mine_2)
    y[1] = gate(y[1], added)
    acc, added = add(
        mine_1, swap_1, x[1], y[1], acc, lag((mine_2,), 0.1, tokens), COSTS[1]
    )

    got = lag((last, swap_2, added), LAGS[1], tokens)
    mine_3 = jnp.where(after(end, got), last, far_2)
    cut = sub * 2 // 3
    parts = [(mine_3[:cut], 0, cut), (mine_3[cut:sub], cut, sub - cut)]
    x[3] = [across_col(part) for part, _, _ in parts]
    y[3] = [across_row(part) for part, _, _ in parts]
    swap_3 = other_core(mine_3)
    y[2] = gate(y[2], added)
    acc, _ = add(
        mine_2, swap_2, x[2], y[2], acc, lag((mine_3,), 0.1, tokens), COSTS[2]
    )

    weight = weigh(mine_3)
    rights = {"own": (mine_3, 0, 0, sub), "swap": (swap_3, 1, 0, sub)}
    lefts = {"own": (mine_3, 0, 0, sub)}
    jobs = (("own", "own"), ("swap", "own"))
    state = finish(
        place, weight, rights, lefts, ("own",), jobs, (acc, None, None)
    )
    for n, (_, first, size) in enumerate(parts):
        acc, out, weighted = state
        token = lag((acc,), 0.1, tokens)
        left, right = gate(x[3][n], token), gate(y[3][n], token)
        here = after(place, lag((left, right), 16.0, tokens))
        rights[f"y{n}"] = (right, 2, first, size)
        rights[f"s{n}"] = (other_core(right), 3, first, size)
        lefts[f"x{n}"] = (left, 1, first, size)
        state = acc, weighted, out
        if n == 0:
            jobs = (("own", "x0"), ("swap", "x0"), ("y0", "own"), ("y0", "x0"))
            jobs += (("s0", "own"), ("s0", "x0"))
            state = finish(here, weight, rights, lefts, ("x0",), jobs, state)
        else:
            jobs = (("own", "x1"), ("swap", "x1"), ("y1", "own"), ("y1", "x0"))
            jobs += (("y1", "x1"), ("y0", "x1"), ("s0", "x1"))
            jobs += (("s1", "own"), ("s1", "x0"), ("s1", "x1"))
            _, out, _ = finish(
                here, weight, rights, lefts, ("x1",), jobs, state, tokens
            )
    return out.reshape(1, 4, 1, sub, 2 * sub)


def solution(mesh):
    in_specs = (P(("row", "col"), "freq"), P("freq"), P("freq"), P(), P(), P("freq"))
    out_specs = P("freq", None, "col", None, "row")
    shape = tuple(mesh.shape[axis] for axis in ("freq", "row", "col"))
    per_device = line_device if shape == (4, 4, 2) else ring_device
    return jax.shard_map(
        per_device, mesh=mesh, in_specs=in_specs, out_specs=out_specs, check_vma=False
    )
```
